256 devices in a mesh: sample: 16 (over x_hi, y, core), tensor: 16 (over z, x_lo).
Axes of the slice: x: 4 (x_hi: 2, x_lo: 2; x = x_hi * 2 + x_lo), y: 4, z: 8, core: 2. Of those that a mesh axis runs over, the one named last changes fastest.
Arguments:
- response_hidden: bfloat16 [1024, 8192], P('sample', 'tensor'), may hold values from -6 to 6, as said below
- prompt_hidden: bfloat16 [4096, 8192], P('sample', 'tensor'), may hold values from -6 to 6
- norm_gain: bfloat16 [8192], replicated, may hold values from 0.099609375 to 1.8984375
- query_weight: bfloat16 [8192, 4096], P(None, 'tensor'), may hold values from -16 to 16
- key_weight: bfloat16 [8192, 512], P(None, 'tensor'), may hold values from -16 to 16
- value_weight: bfloat16 [8192, 512], P(None, 'tensor'), may hold values from -0.0625 to 0.0625
- output_weight: bfloat16 [4096, 8192], P('tensor'), may hold values from -1 to 1
- response_lengths: int32 [16], P('sample'), may hold values from 8 to 64, as said below
- prompt_length: int32 [1], replicated, may hold values from 2048 to 4096
Outputs:
- mixed: bfloat16 [1024, 8192], P('sample', 'tensor')
The draws below stay inside these ranges and needn't reach their ends.
Inputs may be any that keep to these rules, and one draw needn't show every extreme that they name: `response_hidden`: activations. `response_lengths`: some response has all 64 rows live in every draw.
All inputs are finite; a program needn't handle non-finite values.
Results may differ from the reference program's by a relative error of at most 0.025.
Values may be sent and summed in bfloat16 or wider, within the bound.
No kernel may reach another device: no remote copies, remote signals or barrier semaphores. Data moves between devices by JAX's collectives and lax.ppermute only.
A program may use at most 320 MiB of HBM per device.

```python
import jax
import jax.numpy as jnp
from jax import lax

D = 8192
HEAD_DIM = 128
HEADS_DEV = 2
GROUP = 8
RESP = 64
HEADS = 32
KV_HEADS = 4
SAMPLES = 16
PROMPT = 4096
RESP_TOK = 1024
N_TENSOR = 16


def draw_key_weight(key, part):
    key = jax.random.fold_in(key, 11)
    own_dirs = jax.random.normal(key, (D, KV_HEADS * HEAD_DIM), jnp.float32)
    values = own_dirs
    return jnp.clip(values * D ** (-0.5), -16.0, 16.0).astype(jnp.bfloat16)


def draw_query_weight(key, part):
    key = jax.random.fold_in(key, 12)
    own_dirs = jax.random.normal(key, (D, HEADS * HEAD_DIM), jnp.float32)
    values = 2.0 * own_dirs
    return jnp.clip(values * D ** (-0.5), -16.0, 16.0).astype(jnp.bfloat16)


def draw_response_hidden(key, part):
    key = jax.random.fold_in(key, 13)
    base_rows = jax.random.normal(key, (RESP_TOK, D), jnp.float32)
    values = base_rows
    return jnp.clip(values, -6.0, 6.0).astype(jnp.bfloat16)


def draw_response_lengths(key, part):
    key = jax.random.fold_in(key, 14)
    lengths = jax.random.randint(jax.random.fold_in(key, 1), (SAMPLES,), RESP // 8, RESP + 1, jnp.int32)
    full_index = jax.random.randint(jax.random.fold_in(key, 2), (), 0, SAMPLES, jnp.int32)
    return lengths.at[full_index].set(RESP)


def raised(values, key, source, target, blocks, factor):
    def block_of(position):
        return (jnp.arange(values.shape[position]) // (values.shape[position] // blocks)).reshape((-1,) + (1,) * (values.ndim - 1 - position))

    near = jax.random.permutation(key, blocks)[block_of(target)]
    far = (block_of(target) + blocks // 2) % blocks
    return jnp.where((block_of(source) == near) | (block_of(source) == far), factor * values, values)


def level_of(rng, dims, shards, least, high):
    loudness = 1.0
    for axis_at, shards_of in shards:
        draws = jax.random.uniform(jax.random.fold_in(jax.random.fold_in(rng, 6), axis_at), (shards_of,), jnp.float32, least / len(shards), high / len(shards))
        loudness = loudness * jnp.repeat(jnp.exp(draws), dims[axis_at] // shards_of).reshape((-1,) + (1,) * (len(dims) - 1 - axis_at))
    return loudness


def noise(stream_key, shape, scale, most, shards=(), held_as=jnp.bfloat16):
    array = scale * jax.random.normal(stream_key, shape, jnp.float32)
    if shards:
        array = array * level_of(stream_key, shape, shards, -0.22, 0.18)
    return jnp.clip(array, -most, most).astype(held_as)


def gaussian_with(own_key, extent, deviation, limit, cuts, heavy, held_as=jnp.bfloat16):
    entries = deviation * jax.random.normal(own_key, extent, jnp.float32)
    if cuts:
        entries = entries * level_of(own_key, extent, cuts, -0.22, 0.18)
    return jnp.clip(raised(entries, jax.random.fold_in(own_key, 3), *heavy), -limit, limit).astype(held_as)


def setup_inputs(seed: int = 0) -> dict:
    arg_keys = jax.random.split(jax.random.key(seed), 10)
    return {
        "response_hidden": draw_response_hidden(jax.random.fold_in(arg_keys[9], 71), 0),
        "prompt_hidden": noise(arg_keys[1], (PROMPT, D), 1.0, 6.0, ((0, 16), (1, 16))),
        "norm_gain": jnp.clip(1.0 + 0.18 * jax.random.normal(arg_keys[2], (D,), jnp.float32), 0.099609375, 1.8984375).astype(jnp.bfloat16),
        "query_weight": draw_query_weight(jax.random.fold_in(arg_keys[9], 71), 0),
        "key_weight": draw_key_weight(jax.random.fold_in(arg_keys[9], 71), 0),
        "value_weight": noise(arg_keys[5], (D, KV_HEADS * HEAD_DIM), D ** -0.5, 0.0625, ((1, 16),)),
        "output_weight": gaussian_with(arg_keys[6], (HEADS * HEAD_DIM, D), (HEADS * HEAD_DIM // 64) ** -0.5, 1.0, ((0, 16),), (0, 1, 16, 2.0)),
        "response_lengths": draw_response_lengths(jax.random.fold_in(arg_keys[9], 71), 0),
        "prompt_length": jax.random.randint(arg_keys[8], (1,), PROMPT // 2, PROMPT + 1).astype(jnp.int32),
    }


epsilon = 1e-05
rope_base = 500000.0
neg_big = -1e+30

def rms_norm(row_data, gain):
    values = row_data.astype(jnp.float32)
    factor = lax.rsqrt(lax.optimization_barrier(jnp.mean(values * values, axis=1, keepdims=True)) + epsilon)
    return (values * factor * gain.astype(jnp.float32)[None, :]).astype(jnp.bfloat16)

def rotate(values, positions):
    head_width = values.shape[-1]
    half_width = head_width // 2
    inverse = rope_base ** (-(jnp.arange(half_width).astype(jnp.float32) * 2.0 / head_width))
    angles = positions.astype(jnp.float32)[:, None] * inverse[None, :]
    cosine = jnp.cos(angles)[:, None, :]
    sine_part = jnp.sin(angles)[:, None, :]
    first_half = values[..., :half_width]
    second_half = values[..., half_width:]
    return jnp.concatenate([first_half * cosine - second_half * sine_part, second_half * cosine + first_half * sine_part], axis=-1)

def widen(values):
    return lax.optimization_barrier(values.astype(jnp.bfloat16)).astype(jnp.float32)

def by_head(values, row_count):
    return jnp.transpose(values.reshape(row_count, HEAD_DIM, KV_HEADS), (0, 2, 1))

def reference(response_hidden, prompt_hidden, norm_gain, query_weight, key_weight, value_weight, output_weight, response_lengths, prompt_length):
    prompt_size = prompt_length[0]
    normed_prompt = rms_norm(prompt_hidden, norm_gain)
    prompt_raw = jnp.dot(normed_prompt, key_weight, preferred_element_type=jnp.float32)
    prompt_vals = jnp.dot(normed_prompt, value_weight, preferred_element_type=jnp.float32).astype(jnp.bfloat16)
    prompt_positions = jnp.arange(PROMPT, dtype=jnp.int32)
    prompt_keys = rotate(by_head(widen(prompt_raw), PROMPT), prompt_positions).astype(jnp.bfloat16)
    prompt_vals = by_head(prompt_vals, PROMPT)
    row_ids = jnp.arange(RESP, dtype=jnp.int32)
    causal = row_ids[None, :] <= row_ids[:, None]
    prompt_live = jnp.broadcast_to((prompt_positions < prompt_size)[None, :], (RESP, PROMPT))
    allowed = jnp.concatenate([prompt_live, causal], axis=1)
    response_positions = prompt_size + row_ids
    score_scale = HEAD_DIM ** (-0.5)
    out_groups = output_weight.reshape(N_TENSOR, HEADS_DEV * HEAD_DIM, D).astype(jnp.float32)

    def one_response(inputs):
        hidden, length = inputs
        normed = rms_norm(hidden, norm_gain)
        queries = jnp.dot(normed, query_weight, preferred_element_type=jnp.float32).reshape(RESP, HEADS, HEAD_DIM)
        queries = rotate(queries, response_positions).astype(jnp.bfloat16)
        keys_raw = jnp.dot(normed, key_weight, preferred_element_type=jnp.float32)
        own_keys = rotate(by_head(widen(keys_raw), RESP), response_positions).astype(jnp.bfloat16)
        own_vals = jnp.dot(normed, value_weight, preferred_element_type=jnp.float32).astype(jnp.bfloat16)
        own_vals = by_head(own_vals, RESP)
        key_rows = jnp.concatenate([prompt_keys, own_keys], axis=0).astype(jnp.float32)
        value_rows = jnp.concatenate([prompt_vals, own_vals], axis=0).astype(jnp.float32)
        grouped = queries.astype(jnp.float32).reshape(RESP, KV_HEADS, GROUP, HEAD_DIM)
        scores = jnp.einsum('rkgd,skd->kgrs', grouped, key_rows) * score_scale
        scores = jnp.where(allowed[None, None], scores, neg_big)
        row_max = lax.optimization_barrier(jnp.max(scores, axis=-1, keepdims=True))
        weights = jnp.where(allowed[None, None], jnp.exp(scores - row_max), 0.0)
        row_total = lax.optimization_barrier(jnp.sum(weights, axis=-1))
        mixed_vals = jnp.einsum('kgrs,skd->rkgd', widen(weights), value_rows)
        attention = (mixed_vals / jnp.transpose(row_total, (2, 0, 1))[..., None]).astype(jnp.bfloat16)
        attention = attention.reshape(RESP, N_TENSOR, HEADS_DEV * HEAD_DIM).astype(jnp.float32)
        partial_value = widen(jnp.einsum('rtc,tcd->trd', attention, out_groups))
        summed = lax.optimization_barrier(jnp.sum(partial_value, axis=0))
        live_rows = row_ids < length
        return jnp.where(live_rows[:, None], summed, 0.0).astype(jnp.bfloat16)
    results = lax.map(one_response, (response_hidden.reshape(SAMPLES, RESP, D), response_lengths))
    return results.reshape(RESP_TOK, D)
```

```python
import functools

import jax
import jax.numpy as jnp
from jax import lax
from jax.experimental import pallas as pl
from jax.experimental.pallas import tpu as pltpu
from jax.sharding import Mesh
from jax.sharding import PartitionSpec as P

PARTS = (("xh", 2), ("y", 4), ("core", 2), ("k", 4), ("zl", 2), ("xl", 2))
SAMPLE = ("xh", "y", "core")
TENSOR = ("k", "zl", "xl")
ZRING = ("k", "zl")
OWN_HEAD = ("zl", "xl")
KEY_GROUP = ("xh", "core", "zl", "xl")
QUERY_GROUP = "y"

D = 8192
BLOCK = 512
HEAD_DIM = 128
HALF = 64
RESP = 64
PROMPT_ROWS = 256
ROWS = 80
SENT_ROWS = 96
EPSILON = 1e-05
ROPE_BASE = 500000.0
NEG_BIG = -1e30
F32 = jnp.float32
BF16 = jnp.bfloat16
VMEM_LIMIT = 48 * 1024 * 1024


def iota(shape, dim):
    return lax.broadcasted_iota(jnp.int32, shape, dim)


def dot_t(a, b):
    return lax.dot_general(a, b, (((1,), (1,)), ((), ())), preferred_element_type=F32)


def dot(a, b):
    return lax.dot_general(a, b, (((1,), (0,)), ((), ())), preferred_element_type=F32)


def params():
    return pltpu.CompilerParams(vmem_limit_bytes=VMEM_LIMIT)


def pack_kernel(core_ref, key_ref, value_ref, out_ref):
    core = core_ref[0]
    row, col = iota((32, 64), 0), iota((32, 64), 1)
    source = ((row >> 3) & 1) * 32 + (row & 7) * 4 + 2 * core + (row >> 4)
    pick = jnp.where(col == source, 1.0, 0.0).astype(BF16)
    both = jnp.concatenate([key_ref[...], value_ref[...]], axis=0)
    for i in range(out_ref.shape[0]):
        out_ref[i] = dot(pick, both[:, i * BLOCK : (i + 1) * BLOCK]).astype(BF16)


def pack_weights(core, key_rows, value_rows):
    steps = 2
    each = 16 // steps
    return pl.pallas_call(
        pack_kernel,
        grid=(steps,),
        in_specs=[
            pl.BlockSpec(memory_space=pltpu.SMEM),
            pl.BlockSpec((32, each * BLOCK), lambda i: (0, i)),
            pl.BlockSpec((32, each * BLOCK), lambda i: (0, i)),
        ],
        out_specs=pl.BlockSpec((each, 32, BLOCK), lambda i: (i, 0, 0)),
        out_shape=jax.ShapeDtypeStruct((16, 32, BLOCK), BF16),
        compiler_params=params(),
        name="pack_weights",
    )(core, key_rows, value_rows)


def partial_kernel(t_ref, weight_ref, prompt_ref, resp_ref, gain_ref, out_ref, scaled, high, low, sums):
    @pl.when(pl.program_id(0) == 0)
    def _():
        gain = gain_ref[t_ref[0]]
        high[320:384] = jnp.zeros((64, BLOCK), BF16)
        low[320:384] = jnp.zeros((64, BLOCK), BF16)

        def put(at, count, values):
            values = values.astype(F32)
            scaled[at : at + count] = (values * gain).astype(BF16)
            square = values * values
            top = square.astype(BF16)
            high[at : at + count] = top
            low[at : at + count] = (square - top.astype(F32)).astype(BF16)

        for c in range(4):
            put(80 * c, 64, prompt_ref[64 * c : 64 * c + 64])
            put(80 * c + 64, 16, resp_ref[16 * c : 16 * c + 16])
        ones = jnp.ones((16, BLOCK), BF16)
        row = iota((16, 128), 0)
        for c in range(4):
            total = dot_t(ones, high[80 * c : 80 * c + 128]) + dot_t(ones, low[80 * c : 80 * c + 128])
            top = total.astype(BF16).astype(F32)
            rest = total - top
            rows = jnp.where(row == 0, top, jnp.where(row == 1, rest, 0.0))
            sums[c, :, :128] = rows.astype(BF16)
            sums[c, :, 128:] = jnp.zeros((16, 128), BF16)

    weights = weight_ref[0].reshape(256, BLOCK)
    raw = dot_t(scaled[...], weights).astype(BF16)
    row, col = iota((256, 256), 0), iota((256, 256), 1)
    target = ((row >> 3) & 1) * 128 + (row >> 4) * 8 + (row & 7)
    pick = jnp.where(col == target, 1.0, 0.0).astype(BF16)
    ordered = dot(raw, pick).astype(BF16)
    for c in range(4):
        out_ref[c, :ROWS] = ordered[ROWS * c : ROWS * c + ROWS]
        out_ref[c, ROWS:] = sums[c]


def partial_products(t, weights, prompt, resp, gain):
    return pl.pallas_call(
        partial_kernel,
        grid=(4,),
        in_specs=[
            pl.BlockSpec(memory_space=pltpu.SMEM),
            pl.BlockSpec((1, 16, 16, BLOCK), lambda k: (k // 2, 0, k % 2, 0)),
            pl.BlockSpec((PROMPT_ROWS, BLOCK), lambda k: (0, 0)),
            pl.BlockSpec((RESP, BLOCK), lambda k: (0, 0)),
            pl.BlockSpec((16, 1, BLOCK), lambda k: (0, 0, 0)),
        ],
        out_specs=pl.BlockSpec((4, SENT_ROWS, 256), lambda k: (k, 0, 0)),
        out_shape=jax.ShapeDtypeStruct((16, SENT_ROWS, 256), BF16),
        scratch_shapes=[
            pltpu.VMEM((320, BLOCK), BF16),
            pltpu.VMEM((384, BLOCK), BF16),
            pltpu.VMEM((384, BLOCK), BF16),
            pltpu.VMEM((4, 16, 256), BF16),
        ],
        compiler_params=params(),
        name="partial_products",
    )(t, weights, prompt, resp, gain)


def turn(values, cosine, sine):
    return values * cosine + pltpu.roll(values, HALF, 1) * sine


def finish_kernel(parts_ref, cos_ref, sin_ref, out_ref):
    total = jnp.sum(parts_ref[...].astype(F32), axis=0)
    sums = total[ROWS : ROWS + 1, :128] + total[ROWS + 1 : ROWS + 2, :128]
    diagonal = iota((ROWS, 128), 0) == iota((ROWS, 128), 1)
    column = jnp.sum(jnp.where(diagonal, jnp.broadcast_to(sums, (ROWS, 128)), 0.0), axis=1, keepdims=True)
    factor = lax.rsqrt(column * (1.0 / D) + EPSILON)
    scaled = total[:ROWS] * factor
    keys = turn(scaled[:, :HEAD_DIM], cos_ref[...], sin_ref[...])
    out_ref[:, :HEAD_DIM] = keys.astype(BF16)
    out_ref[:, HEAD_DIM:] = scaled[:, HEAD_DIM:].astype(BF16)


def finish_keys(parts, cosine, sine):
    return pl.pallas_call(
        finish_kernel,
        out_shape=jax.ShapeDtypeStruct((ROWS, 256), BF16),
        compiler_params=params(),
        name="finish_keys",
    )(parts, cosine, sine)


def query_kernel(index_ref, hidden_ref, weight_ref, gain_ref, cos_ref, sin_ref, out_ref, total, squares):
    step = pl.program_id(0)

    @pl.when(step == 0)
    def _():
        total[...] = jnp.zeros_like(total)
        squares[...] = jnp.zeros_like(squares)

    for j in range(2):
        hidden = hidden_ref[0, j].astype(F32)
        scaled = (hidden * gain_ref[j]).astype(BF16)
        total[...] += dot(scaled, weight_ref[j * BLOCK : (j + 1) * BLOCK])
        squares[...] += jnp.sum(hidden * hidden, axis=1, keepdims=True)

    @pl.when(step == pl.num_programs(0) - 1)
    def _():
        factor = lax.rsqrt(squares[...] * (1.0 / D) + EPSILON)
        for h in range(2):
            part = slice(h * HEAD_DIM, (h + 1) * HEAD_DIM)
            query = turn(total[:, part] * factor, cos_ref[...], sin_ref[...])
            out_ref[:, part] = query.astype(BF16)


def queries_of(index, hidden, weight, gain, cosine, sine):
    return pl.pallas_call(
        query_kernel,
        grid_spec=pltpu.PrefetchScalarGridSpec(
            num_scalar_prefetch=1,
            grid=(8,),
            in_specs=[
                pl.BlockSpec((1, 2, RESP, BLOCK), lambda i, index: (i, 0, 0, 0)),
                pl.BlockSpec((2 * BLOCK, 256), lambda i, index: (index[i], 0)),
                pl.BlockSpec((2, 1, BLOCK), lambda i, index: (index[i], 0, 0)),
                pl.BlockSpec((RESP, HEAD_DIM), lambda i, index: (0, 0)),
                pl.BlockSpec((RESP, HEAD_DIM), lambda i, index: (0, 0)),
            ],
            out_specs=pl.BlockSpec((RESP, 256), lambda i, index: (0, 0)),
            scratch_shapes=[pltpu.VMEM((RESP, 256), F32), pltpu.VMEM((RESP, 1), F32)],
        ),
        out_shape=jax.ShapeDtypeStruct((RESP, 256), BF16),
        compiler_params=params(),
        name="queries",
    )(index, hidden, weight, gain, cosine, sine)


def attend_kernel(info_ref, query_ref, rows_ref, out_ref):
    own_y, own_place, length = info_ref[0], info_ref[1], info_ref[2]
    rows = rows_ref[...].reshape(16, ROWS, 256)
    prompt = rows[:, :64].reshape(1024, 256)
    prompt_keys, prompt_values = prompt[:, :HEAD_DIM], prompt[:, HEAD_DIM:]
    own = rows_ref[own_place]
    own = own[:, 64:].reshape(RESP, 256)
    own_keys, own_values = own[:, :HEAD_DIM], own[:, HEAD_DIM:]
    scale = HEAD_DIM ** (-0.5)

    column = iota((1, 1024), 1)
    place = column >> 8
    sample = (place >> 1) * 8 + own_y * 2 + (place & 1)
    live = sample * PROMPT_ROWS + (column & 255) < length
    causal = iota((RESP, RESP), 1) <= iota((RESP, RESP), 0)
    lane = iota((RESP, 128), 1)

    for y in range(4):
        mine = jnp.logical_and(causal, own_y == y)
        extra = jnp.zeros((RESP, 128), F32)
        for h in range(2):
            part = slice(h * HEAD_DIM, (h + 1) * HEAD_DIM)
            query = query_ref[y, :, part]
            far = jnp.where(live, dot_t(query, prompt_keys) * scale, NEG_BIG)
            near = jnp.where(mine, dot_t(query, own_keys) * scale, NEG_BIG)
            top = jnp.maximum(jnp.max(far, axis=1, keepdims=True), jnp.max(near, axis=1, keepdims=True))
            far = jnp.where(live, jnp.exp(far - top), 0.0)
            near = jnp.where(mine, jnp.exp(near - top), 0.0)
            total = jnp.sum(far, axis=1, keepdims=True) + jnp.sum(near, axis=1, keepdims=True)
            summed = dot(far.astype(BF16), prompt_values) + dot(near.astype(BF16), own_values)
            some = total > 0.0
            safe = jnp.where(some, total, 1.0)
            out_ref[y, :, part] = (summed / safe).astype(BF16)
            level = jnp.where(some, top + jnp.log(safe), NEG_BIG)
            first = level.astype(BF16).astype(F32)
            rest = level - first
            second = rest.astype(BF16).astype(F32)
            third = rest - second
            for i, piece in enumerate((first, second, third)):
                extra = jnp.where(lane == 3 * h + i, piece, extra)
        out_ref[y, :, 256:] = extra.astype(BF16)


def attend(info, queries, rows):
    return pl.pallas_call(
        attend_kernel,
        in_specs=[
            pl.BlockSpec(memory_space=pltpu.SMEM),
            pl.BlockSpec(memory_space=pltpu.VMEM),
            pl.BlockSpec(memory_space=pltpu.VMEM),
        ],
        out_shape=jax.ShapeDtypeStruct((4, RESP, 384), BF16),
        compiler_params=params(),
        name="attend",
    )(info, queries, rows)


def project_kernel(parts_ref, weight_ref, out_ref, attention):
    @pl.when(pl.program_id(0) == 0)
    def _():
        lane = iota((RESP, 128), 1)
        extras = [parts_ref[y, :, 256:].astype(F32) for y in range(4)]
        for h in range(2):
            part = slice(h * HEAD_DIM, (h + 1) * HEAD_DIM)
            mine = jnp.logical_and(lane >= 3 * h, lane < 3 * h + 3)
            levels = [jnp.sum(jnp.where(mine, e, 0.0), axis=1, keepdims=True) for e in extras]
            top = functools.reduce(jnp.maximum, levels)
            shares = [jnp.exp(level - top) for level in levels]
            total = functools.reduce(jnp.add, shares)
            summed = functools.reduce(jnp.add, [s * parts_ref[y, :, part].astype(F32) for y, s in enumerate(shares)])
            attention[:, part] = (summed / total).astype(BF16)

    for j in range(out_ref.shape[0]):
        out_ref[j] = dot(attention[...], weight_ref[:, j * BLOCK : (j + 1) * BLOCK]).astype(BF16)


def project(parts, weight):
    steps = 4
    each = 16 // steps
    return pl.pallas_call(
        project_kernel,
        grid=(steps,),
        in_specs=[
            pl.BlockSpec((4, RESP, 384), lambda i: (0, 0, 0)),
            pl.BlockSpec((256, each * BLOCK), lambda i: (0, i)),
        ],
        out_specs=pl.BlockSpec((each, RESP, BLOCK), lambda i: (i, 0, 0)),
        out_shape=jax.ShapeDtypeStruct((16, RESP, BLOCK), BF16),
        scratch_shapes=[pltpu.VMEM((RESP, 256), BF16)],
        compiler_params=params(),
        name="project",
    )(parts, weight)


def swap(values, axis):
    return lax.all_to_all(values, axis, 0, 0, tiled=False)


def share(values, axis, count):
    return swap(jnp.broadcast_to(values[None], (count,) + values.shape), axis)


def ring(hidden):
    other = lax.ppermute(hidden, "xl", [(0, 1), (1, 0)])
    first = lax.axis_index("xl") == 0
    pair = jnp.stack([jnp.where(first, hidden, other), jnp.where(first, other, hidden)])
    onward = [(i, (i + 1) % 8) for i in range(8)]
    back = [(i, (i + 7) % 8) for i in range(8)]
    z = lax.axis_index(ZRING)
    blocks, index = [pair], [z]
    up = down = pair
    for step in range(1, 5):
        up = lax.ppermute(up, ZRING, onward)
        blocks.append(up)
        index.append((z + 8 - step) % 8)
        if step < 4:
            down = lax.ppermute(down, ZRING, back)
            blocks.append(down)
            index.append((z + step) % 8)
    return jnp.stack(index).astype(jnp.int32), jnp.stack(blocks)


def body(
    response_hidden,
    prompt_hidden,
    norm_gain,
    query_weight,
    key_weight,
    value_weight,
    output_weight,
    response_lengths,
    prompt_length,
):
    length = prompt_length[0]
    core, y = lax.axis_index("core"), lax.axis_index("y")
    sample, quarter = lax.axis_index(SAMPLE), lax.axis_index(OWN_HEAD)
    gain = norm_gain.astype(F32).reshape(16, 1, BLOCK)

    row = jnp.arange(144, dtype=jnp.int32)
    positions = jnp.where(
        row < 64,
        sample * PROMPT_ROWS + quarter * 64 + row,
        jnp.where(row < 80, length + quarter * 16 + row - 64, length + row - 80),
    )
    lane = jnp.arange(HEAD_DIM, dtype=jnp.int32)
    inverse = ROPE_BASE ** (-((lane % HALF).astype(F32) * 2.0 / HEAD_DIM))
    angles = positions.astype(F32)[:, None] * inverse[None, :]
    cosine = jnp.cos(angles)
    sine = jnp.sin(angles) * jnp.where(lane < HALF, -1.0, 1.0)[None, :]

    index, hidden = ring(response_hidden)

    packed = pack_weights(core.reshape(1), key_weight.T, value_weight.T)
    half = swap(packed, TENSOR)
    other = lax.ppermute(half, "core", [(0, 1), (1, 0)])
    weights = jnp.stack([jnp.where(core == 0, half, other), jnp.where(core == 0, other, half)])

    partial_kv = partial_products(
        lax.axis_index(TENSOR).reshape(1), weights, prompt_hidden, response_hidden, gain
    )
    rows = finish_keys(swap(partial_kv, TENSOR), cosine[:80], sine[:80])
    rows = share(rows, KEY_GROUP, 16).reshape(4, 4, ROWS, 256)

    queries = queries_of(index, hidden, query_weight, gain, cosine[80:], sine[80:])
    queries = share(queries, QUERY_GROUP, 4)

    place = lax.axis_index(("xh", "core"))
    info = jnp.stack([y, place, length]).astype(jnp.int32)
    parts = swap(attend(info, queries, rows), QUERY_GROUP)
    partial = project(parts, output_weight)
    summed = jnp.sum(swap(partial, TENSOR).astype(F32), axis=0)
    live = jnp.arange(RESP, dtype=jnp.int32) < response_lengths[0]
    return jnp.where(live[:, None], summed, 0.0).astype(BF16)


def solution(mesh):
    names = tuple(name for name, _ in PARTS)
    sizes = tuple(size for _, size in PARTS)
    fine = Mesh(mesh.devices.reshape(sizes), names)
    return jax.shard_map(
        body,
        mesh=fine,
        in_specs=(
            P(SAMPLE, TENSOR),
            P(SAMPLE, TENSOR),
            P(),
            P(None, TENSOR),
            P(None, TENSOR),
            P(None, TENSOR),
            P(TENSOR, None),
            P(SAMPLE),
            P(),
        ),
        out_specs=P(SAMPLE, TENSOR),
        check_vma=False,
    )
```

```python
import functools
import math

import jax
import jax.numpy as jnp
from jax import lax
from jax.experimental import pallas as pl
from jax.experimental.pallas import tpu as pltpu
from jax.sharding import Mesh
from jax.sharding import PartitionSpec as P

PARTS = (("xh", 2), ("y", 4), ("core", 2), ("k", 4), ("zl", 2), ("xl", 2))
SAMPLE = ("xh", "y", "core")
TENSOR = ("k", "zl", "xl")
ZRING = ("k", "zl")
OWN_HEAD = ("zl", "xl")
KEY_GROUP = ("xh", "core", "zl", "xl")

D = 8192
BLOCK = 512
HEAD_DIM = 128
HALF = 64
RESP = 64
PROMPT_ROWS = 256
ROWS = 80
SENT_ROWS = 2 * ROWS + 16
EPSILON = 1e-05
ROPE_BASE = 500000.0
NEG_BIG = -1e30
CORE_AT, XL_AT, T_AT, Y_AT, PLACE_AT, LENGTH_AT, Z_AT = 0, 1, 2, 3, 4, 5, 6
RING = (0, 7, 1, 6, 2, 5, 3, 4)
F32 = jnp.float32
BF16 = jnp.bfloat16
SMALL = 12 * 1024 * 1024


def iota(shape, dim):
    return lax.broadcasted_iota(jnp.int32, shape, dim)


def dot_t(a, b):
    return lax.dot_general(a, b, (((1,), (1,)), ((), ())), preferred_element_type=F32)


def dot(a, b):
    return lax.dot_general(a, b, (((1,), (0,)), ((), ())), preferred_element_type=F32)


def params(limit=None):
    return pltpu.CompilerParams(vmem_limit_bytes=limit)


def pack_kernel(info_ref, key_ref, value_ref, out_ref):
    row, col = iota((16, 64), 0), iota((16, 64), 1)
    source = (row >> 3) * 32 + (row & 7) * 4 + info_ref[0]
    pick = jnp.where(col == source, 1.0, 0.0).astype(BF16)
    both = jnp.concatenate([key_ref[...], value_ref[...]], axis=0)
    for i in range(out_ref.shape[0]):
        out_ref[i] = dot(pick, both[:, i * BLOCK : (i + 1) * BLOCK]).astype(BF16)


def pack_weights(head, key_rows, value_rows):
    steps = 2
    each = 16 // steps
    return pl.pallas_call(
        pack_kernel,
        grid=(steps,),
        in_specs=[
            pl.BlockSpec(memory_space=pltpu.SMEM),
            pl.BlockSpec((32, each * BLOCK), lambda i: (0, i)),
            pl.BlockSpec((32, each * BLOCK), lambda i: (0, i)),
        ],
        out_specs=pl.BlockSpec((each, 16, BLOCK), lambda i: (i, 0, 0)),
        out_shape=jax.ShapeDtypeStruct((16, 16, BLOCK), BF16),
        compiler_params=params(),
        name="pack_weights",
    )(head, key_rows, value_rows)


def scale_kernel(info_ref, prompt_ref, resp_ref, gain_ref, scaled, sums, high, low):
    gain = gain_ref[info_ref[T_AT]]
    high[320:384] = jnp.zeros((64, BLOCK), BF16)
    low[320:384] = jnp.zeros((64, BLOCK), BF16)

    def put(at, count, values):
        values = values.astype(F32)
        scaled[at : at + count] = (values * gain).astype(BF16)
        square = values * values
        top = square.astype(BF16)
        high[at : at + count] = top
        low[at : at + count] = (square - top.astype(F32)).astype(BF16)

    for c in range(4):
        put(80 * c, 64, prompt_ref[64 * c : 64 * c + 64])
        put(80 * c + 64, 16, resp_ref[16 * c : 16 * c + 16])
    ones = jnp.ones((16, BLOCK), BF16)
    row = iota((16, 128), 0)
    for c in range(4):
        total = dot_t(ones, high[80 * c : 80 * c + 128]) + dot_t(ones, low[80 * c : 80 * c + 128])
        top = total.astype(BF16).astype(F32)
        rest = total - top
        sums[c] = jnp.where(row == 0, top, jnp.where(row == 1, rest, 0.0)).astype(BF16)


def scale_rows(info, prompt, resp, gain):
    vmem = pl.BlockSpec(memory_space=pltpu.VMEM)
    return pl.pallas_call(
        scale_kernel,
        in_specs=[pl.BlockSpec(memory_space=pltpu.SMEM), vmem, vmem, vmem],
        out_shape=(jax.ShapeDtypeStruct((320, BLOCK), BF16), jax.ShapeDtypeStruct((4, 16, 128), BF16)),
        scratch_shapes=[pltpu.VMEM((384, BLOCK), BF16), pltpu.VMEM((384, BLOCK), BF16)],
        compiler_params=params(SMALL),
        name="scale_rows",
    )(info, prompt, resp, gain)


def partial_kernel(count, heads_ref, scaled_ref, sums_ref, *refs):
    pieces, out_ref = refs[:count], refs[-1]
    for i in range(count):

        @pl.when(pl.program_id(0) == i)
        def _(i=i):
            raw = dot_t(scaled_ref[...], pieces[i][...].reshape(256, BLOCK)).astype(BF16)
            for c in range(4):
                mine = raw[ROWS * c : ROWS * c + ROWS]
                out_ref[c, :ROWS] = mine[:, :128]
                out_ref[c, ROWS : 2 * ROWS] = mine[:, 128:]
                out_ref[c, 2 * ROWS :] = sums_ref[c]


def partial_products(heads, scaled, sums, pieces, before=None):
    def whole(shape):
        return pl.BlockSpec(shape, lambda i, heads: (0,) * len(shape))

    count = len(pieces)
    in_specs = [whole((320, BLOCK)), whole((4, 16, 128))] + [whole((16, 16, BLOCK))] * count
    operands = [heads, scaled, sums, *pieces]
    aliases = {}
    if before is not None:
        in_specs.append(pl.BlockSpec(memory_space=pl.ANY))
        operands.append(before)
        aliases = {len(operands) - 1: 0}
    return pl.pallas_call(
        functools.partial(partial_kernel, count),
        grid_spec=pltpu.PrefetchScalarGridSpec(
            num_scalar_prefetch=1,
            grid=(count,),
            in_specs=in_specs,
            out_specs=pl.BlockSpec((4, SENT_ROWS, 128), lambda i, heads: (heads[i], 0, 0)),
        ),
        out_shape=jax.ShapeDtypeStruct((16, SENT_ROWS, 128), BF16),
        input_output_aliases=aliases,
        compiler_params=params(SMALL),
        name="partial_products",
    )(*operands)


def turn(values, cosine, sine):
    return values * cosine + pltpu.roll(values, HALF, 1) * sine


def finish_kernel(parts_ref, cos_ref, sin_ref, out_ref):
    total = jnp.sum(parts_ref[...].astype(F32), axis=0)
    sums = total[2 * ROWS : 2 * ROWS + 1] + total[2 * ROWS + 1 : 2 * ROWS + 2]
    diagonal = iota((ROWS, 128), 0) == iota((ROWS, 128), 1)
    column = jnp.sum(jnp.where(diagonal, jnp.broadcast_to(sums, (ROWS, 128)), 0.0), axis=1, keepdims=True)
    factor = lax.rsqrt(column * (1.0 / D) + EPSILON)
    raw = jnp.concatenate([total[:ROWS] * factor, total[ROWS : 2 * ROWS] * factor], axis=1).astype(BF16)
    row, col = iota((256, 256), 0), iota((256, 256), 1)
    target = ((row >> 3) & 1) * 128 + (row >> 4) * 8 + (row & 7)
    ordered = dot(raw, jnp.where(col == target, 1.0, 0.0).astype(BF16))
    keys = turn(ordered[:, :HEAD_DIM], cos_ref[:ROWS], sin_ref[:ROWS]).astype(BF16)
    values = ordered[:, HEAD_DIM:].astype(BF16)
    for i in range(out_ref.shape[0]):
        out_ref[i, :, :HEAD_DIM] = keys
        out_ref[i, :, HEAD_DIM:] = values


def finish_keys(parts, cosine, sine):
    return pl.pallas_call(
        finish_kernel,
        out_shape=jax.ShapeDtypeStruct((16, ROWS, 256), BF16),
        compiler_params=params(SMALL),
        name="finish_keys",
    )(parts, cosine, sine)


def query_kernel(info_ref, gain_ref, cos_ref, sin_ref, weight_ref, *refs):
    blocks, (out_ref, weights, hiddens, weight_sems, hidden_sems) = refs[:8], refs[8:]
    xl = info_ref[XL_AT]
    places = [(info_ref[Z_AT] + step) % 8 for step in RING]
    copies = []
    for i, z in enumerate(places):
        rows = pl.ds(pl.multiple_of(z * 2 * BLOCK, 2 * BLOCK), 2 * BLOCK)
        copies.append(
            (
                pltpu.make_async_copy(weight_ref.at[rows], weights.at[i], weight_sems.at[i]),
                pltpu.make_async_copy(blocks[i], hiddens.at[i], hidden_sems.at[i]),
            )
        )
    for copy in copies:
        copy[0].start()
        copy[1].start()
    total = jnp.zeros((RESP, 256), F32)
    squares = jnp.zeros((RESP, 1), F32)
    for i, z in enumerate(places):
        copies[i][0].wait()
        copies[i][1].wait()
        for j in range(2):
            x = j ^ xl
            hidden = hiddens[i, j].astype(F32)
            scaled = (hidden * gain_ref[2 * z + x]).astype(BF16)
            total += dot(scaled, weights[i, pl.ds(pl.multiple_of(x * BLOCK, BLOCK), BLOCK)])
            squares += jnp.sum(hidden * hidden, axis=1, keepdims=True)
    factor = lax.rsqrt(squares * (1.0 / D) + EPSILON)
    for h in range(2):
        part = slice(h * HEAD_DIM, (h + 1) * HEAD_DIM)
        query = turn(total[:, part] * factor, cos_ref[ROWS:], sin_ref[ROWS:])
        out_ref[:, part] = query.astype(BF16)


def queries_of(info, gain, weight, cosine, sine, blocks):
    vmem, anywhere = pl.BlockSpec(memory_space=pltpu.VMEM), pl.BlockSpec(memory_space=pl.ANY)
    return pl.pallas_call(
        query_kernel,
        in_specs=[pl.BlockSpec(memory_space=pltpu.SMEM)] + [vmem] * 3 + [anywhere] * 9,
        out_shape=jax.ShapeDtypeStruct((RESP, 256), BF16),
        scratch_shapes=[
            pltpu.VMEM((8, 2 * BLOCK, 256), BF16),
            pltpu.VMEM((8, 2, RESP, BLOCK), BF16),
            pltpu.SemaphoreType.DMA((8,)),
            pltpu.SemaphoreType.DMA((8,)),
        ],
        compiler_params=params(SMALL),
        name="queries",
    )(info, gain, cosine, sine, weight, *blocks)


def attend_kernel(info_ref, rows_ref, *refs):
    queries, outs = refs[:4], refs[4:]
    own_y = info_ref[Y_AT]
    rows = rows_ref[...].reshape(16, ROWS, 256)
    prompt = rows[:, :64].reshape(1024, 256)
    prompt_keys, prompt_values = prompt[:, :HEAD_DIM], prompt[:, HEAD_DIM:]
    own = rows_ref[info_ref[PLACE_AT]]
    own = own[:, 64:].reshape(RESP, 256)
    own_keys, own_values = own[:, :HEAD_DIM], own[:, HEAD_DIM:]
    scale = HEAD_DIM ** (-0.5)
    power = scale * math.log2(math.e)

    column = iota((1, 1024), 1)
    place = column >> 8
    sample = (place >> 1) * 8 + own_y * 2 + (place & 1)
    live = sample * PROMPT_ROWS + (column & 255) < info_ref[LENGTH_AT]
    causal = iota((2 * RESP, RESP), 1) <= (iota((2 * RESP, RESP), 0) & (RESP - 1))
    lane = iota((RESP, 128), 1)

    for i in range(4):
        query = jnp.concatenate([queries[i][:, :HEAD_DIM], queries[i][:, HEAD_DIM:]], axis=0)
        far = jnp.where(live, dot_t(query, prompt_keys), NEG_BIG)
        top = jnp.max(far, axis=1, keepdims=True)
        if i == 0:
            near = jnp.where(causal, dot_t(query, own_keys), NEG_BIG)
            top = jnp.maximum(top, jnp.max(near, axis=1, keepdims=True))
        top = jnp.maximum(top, 0.5 * NEG_BIG)
        far = jnp.exp2((far - top) * power)
        total = jnp.sum(far, axis=1, keepdims=True)
        summed = dot(far.astype(BF16), prompt_values)
        if i == 0:
            near = jnp.exp2((near - top) * power)
            total += jnp.sum(near, axis=1, keepdims=True)
            summed += dot(near.astype(BF16), own_values)
        some = total > 0.0
        safe = jnp.where(some, total, 1.0)
        result = (summed / safe).astype(BF16)
        level = jnp.where(some, top * scale + jnp.log(safe), NEG_BIG)
        first = level.astype(BF16).astype(F32)
        rest = level - first
        second = rest.astype(BF16).astype(F32)
        third = rest - second
        extra = jnp.zeros((RESP, 128), F32)
        for h in range(2):
            mine = slice(h * RESP, (h + 1) * RESP)
            outs[i][:, h * HEAD_DIM : (h + 1) * HEAD_DIM] = result[mine]
            for n, piece in enumerate((first, second, third)):
                extra = jnp.where(lane == 3 * h + n, piece[mine], extra)
        outs[i][:, 256:] = extra.astype(BF16)


def attend(info, rows, queries):
    vmem = pl.BlockSpec(memory_space=pltpu.VMEM)
    return pl.pallas_call(
        attend_kernel,
        in_specs=[pl.BlockSpec(memory_space=pltpu.SMEM)] + [vmem] * 5,
        out_shape=(jax.ShapeDtypeStruct((RESP, 384), BF16),) * 4,
        compiler_params=params(SMALL),
        name="attend",
    )(info, rows, *queries)


def merge_kernel(*refs):
    parts, out_ref = refs[:4], refs[4]
    lane = iota((RESP, 128), 1)
    extras = [part[:, 256:].astype(F32) for part in parts]
    for h in range(2):
        head = slice(h * HEAD_DIM, (h + 1) * HEAD_DIM)
        mine = jnp.logical_and(lane >= 3 * h, lane < 3 * h + 3)
        levels = [jnp.sum(jnp.where(mine, e, 0.0), axis=1, keepdims=True) for e in extras]
        top = functools.reduce(jnp.maximum, levels)
        shares = [jnp.exp(level - top) for level in levels]
        total = functools.reduce(jnp.add, shares)
        pieces = [share * part[:, head].astype(F32) for share, part in zip(shares, parts)]
        out_ref[:, head] = (functools.reduce(jnp.add, pieces) / total).astype(BF16)


def merge(parts):
    vmem = pl.BlockSpec(memory_space=pltpu.VMEM)
    return pl.pallas_call(
        merge_kernel,
        in_specs=[vmem] * 4,
        out_shape=jax.ShapeDtypeStruct((RESP, 256), BF16),
        compiler_params=params(SMALL),
        name="merge",
    )(*parts)


def z_of(i, info):
    return (4 * info[CORE_AT] + 2 * (info[Y_AT] % 2)) ^ i


def project_kernel(info_ref, own_ref, other_ref, own_weight, *refs):
    cross, out_ref = refs[:4], refs[4]
    for i in range(8):
        result = dot(own_ref[...], own_weight[:, pl.ds(i * BLOCK, BLOCK)])
        result += dot(other_ref[...], cross[i // 2][:, pl.ds((i % 2) * BLOCK, BLOCK)])
        out_ref[z_of(i, info_ref)] = result.astype(BF16)


def project(info, own, other, own_weight, cross):
    vmem = pl.BlockSpec(memory_space=pltpu.VMEM)
    return pl.pallas_call(
        project_kernel,
        in_specs=[pl.BlockSpec(memory_space=pltpu.SMEM)] + [vmem] * 7,
        out_shape=jax.ShapeDtypeStruct((8, RESP, BLOCK), BF16),
        compiler_params=params(SMALL),
        name="project",
    )(info, own, other, own_weight, *cross)


def pick_kernel(info_ref, own_ref, other_ref, out_ref, sent_ref):
    out_ref[...] = own_ref[...]

    @pl.when(pl.program_id(0) < 2)
    def _():
        sent_ref[...] = other_ref[...]


def pick_columns(info, weight):
    def other_at(i, info):
        return 0, 2 * z_of(jnp.minimum(i, 1), info) + 1 - info[XL_AT]

    return pl.pallas_call(
        pick_kernel,
        grid_spec=pltpu.PrefetchScalarGridSpec(
            num_scalar_prefetch=1,
            grid=(8,),
            in_specs=[
                pl.BlockSpec((256, BLOCK), lambda i, info: (0, 2 * z_of(i, info) + info[XL_AT])),
                pl.BlockSpec((256, BLOCK), other_at),
            ],
            out_specs=[
                pl.BlockSpec((256, BLOCK), lambda i, info: (0, i)),
                pl.BlockSpec((256, BLOCK), lambda i, info: (0, jnp.minimum(i, 1))),
            ],
        ),
        out_shape=(
            jax.ShapeDtypeStruct((256, 8 * BLOCK), BF16),
            jax.ShapeDtypeStruct((256, 2 * BLOCK), BF16),
        ),
        compiler_params=params(SMALL),
        name="pick_columns",
    )(info, weight, weight)


def swap(values, axis):
    return lax.all_to_all(values, axis, 0, 0, tiled=False)


def body(
    response_hidden,
    prompt_hidden,
    norm_gain,
    query_weight,
    key_weight,
    value_weight,
    output_weight,
    response_lengths,
    prompt_length,
):
    length = prompt_length[0]
    core, y = lax.axis_index("core"), lax.axis_index("y")
    sample, quarter = lax.axis_index(SAMPLE), lax.axis_index(OWN_HEAD)
    gain = norm_gain.astype(F32).reshape(16, 1, BLOCK)

    row = jnp.arange(144, dtype=jnp.int32)
    positions = jnp.where(
        row < 64,
        sample * PROMPT_ROWS + quarter * 64 + row,
        jnp.where(row < 80, length + quarter * 16 + row - 64, length + row - 80),
    )
    lane = jnp.arange(HEAD_DIM, dtype=jnp.int32)
    inverse = ROPE_BASE ** (-((lane % HALF).astype(F32) * 2.0 / HEAD_DIM))
    angles = positions.astype(F32)[:, None] * inverse[None, :]
    cosine = jnp.cos(angles)
    sine = jnp.sin(angles) * jnp.where(lane < HALF, -1.0, 1.0)[None, :]

    xl, z = lax.axis_index("xl"), lax.axis_index(ZRING)
    info = jnp.stack(
        [core, xl, lax.axis_index(TENSOR), y, lax.axis_index(("xh", "core")), length, z]
    ).astype(jnp.int32)
    flip = [(0, 1), (1, 0)]
    onward = [(i, (i + 1) % 8) for i in range(8)]
    back = [(i, (i + 7) % 8) for i in range(8)]

    def up(values):
        return lax.ppermute(values, ZRING, onward)

    def down(values):
        return lax.ppermute(values, ZRING, back)

    packed = pack_weights(y.reshape(1), key_weight.T, value_weight.T)
    beside = lax.ppermute(response_hidden, "xl", flip)
    weights = swap(packed, TENSOR)
    pair = jnp.stack([response_hidden, beside])
    up1, down1 = up(pair), down(pair)
    four = lax.ppermute(pair, ZRING, [(i, (i + 4) % 8) for i in range(8)])
    scaled, sums = scale_rows(info, prompt_hidden, response_hidden, gain)
    own, sent = pick_columns(info, output_weight)
    weights, pair, scaled, sums, own, sent = lax.optimization_barrier((weights, pair, scaled, sums, own, sent))
    one, two, three = (
        lax.ppermute(weights, "y", [(i, i ^ step) for i in range(4)]) for step in (1, 2, 3)
    )
    first = lax.ppermute(sent, "xl", flip)
    up2, down2 = up(up1), down(down1)
    heads = jnp.stack([y, y ^ 1, y ^ 3]).astype(jnp.int32)
    products = partial_products(heads, scaled, sums, (weights, one, three))
    products = partial_products((y ^ 2).reshape(1), scaled, sums, (two,), products)
    products, up2, down2, first, four = lax.optimization_barrier((products, up2, down2, first, four))
    products = swap(products, TENSOR)
    up3, down3 = up(up2), down(down2)
    second = lax.ppermute(first, "y", [(i, i ^ 1) for i in range(4)])
    products, up3, down3, second = lax.optimization_barrier((products, up3, down3, second))
    blocks = (pair, up1, down1, up2, down2, up3, down3, four)
    queries = queries_of(info, gain, query_weight, cosine, sine, blocks)
    cross = (first, second, lax.ppermute(first, "core", flip), lax.ppermute(second, "core", flip))
    rows = finish_keys(products, cosine, sine)
    rows = swap(rows, KEY_GROUP).reshape(4, 4, ROWS, 256)

    def along(values, step):
        return lax.ppermute(values, "y", [(i, (i + step) % 4) for i in range(4)])

    pooled = [queries] + [along(queries, step) for step in (1, 2, 3)]
    rows, cross = lax.optimization_barrier((rows, cross))
    parts = attend(info, rows, pooled)
    attention = merge([parts[0]] + [along(parts[step], -step) for step in (1, 2, 3)])
    other = lax.ppermute(attention, "xl", flip)
    partial = project(info, attention, other, own, cross)
    summed = jnp.sum(swap(partial, ZRING).astype(F32), axis=0)
    live = jnp.arange(RESP, dtype=jnp.int32) < response_lengths[0]
    return jnp.where(live[:, None], summed, 0.0).astype(BF16)


def solution(mesh):
    names = tuple(name for name, _ in PARTS)
    sizes = tuple(size for _, size in PARTS)
    fine = Mesh(mesh.devices.reshape(sizes), names)
    return jax.shard_map(
        body,
        mesh=fine,
        in_specs=(
            P(SAMPLE, TENSOR),
            P(SAMPLE, TENSOR),
            P(),
            P(None, TENSOR),
            P(None, TENSOR),
            P(None, TENSOR),
            P(TENSOR, None),
            P(SAMPLE),
            P(),
        ),
        out_specs=P(SAMPLE, TENSOR),
        check_vma=False,
    )
```

```python
import functools
import math

import jax
import jax.numpy as jnp
from jax import lax
from jax.experimental import pallas as pl
from jax.experimental.pallas import tpu as pltpu
from jax.sharding import Mesh
from jax.sharding import PartitionSpec as P

PARTS = (("xh", 2), ("y", 4), ("core", 2), ("k", 4), ("zl", 2), ("xl", 2))
SAMPLE = ("xh", "y", "core")
TENSOR = ("k", "zl", "xl")
ZRING = ("k", "zl")
KEY_GROUP = ("xh", "core", "zl", "xl")

D = 8192
BLOCK = 512
HEAD_DIM = 128
HALF = 64
RESP = 64
PROMPT_ROWS = 256
ROWS = 160
SENT_ROWS = ROWS + 16
PACKED = 64 + RESP
EPSILON = 1e-05
ROPE_BASE = 500000.0
NEG_BIG = -1e30
CORE_AT, XL_AT, T_AT, Y_AT, PLACE_AT, LENGTH_AT = 0, 1, 2, 3, 4, 5
F32 = jnp.float32
BF16 = jnp.bfloat16
SMALL = 12 * 1024 * 1024


def iota(shape, dim):
    return lax.broadcasted_iota(jnp.int32, shape, dim)


def dot_t(a, b):
    return lax.dot_general(a, b, (((1,), (1,)), ((), ())), preferred_element_type=F32)


def dot(a, b):
    return lax.dot_general(a, b, (((1,), (0,)), ((), ())), preferred_element_type=F32)


LONG = pl.CostEstimate(flops=30_000_000_000, bytes_accessed=1_000_000, transcendentals=0)


def params(limit=None):
    return pltpu.CompilerParams(vmem_limit_bytes=limit)


def pack_kernel(core_ref, key_ref, value_ref, hidden_ref, out_ref):
    row, col = iota((32, 64), 0), iota((32, 64), 1)
    source = ((row >> 3) & 1) * 32 + (row & 7) * 4 + 2 * core_ref[0] + (row >> 4)
    pick = jnp.where(col == source, 1.0, 0.0).astype(BF16)
    both = jnp.concatenate([key_ref[...], value_ref[...]], axis=0)
    for i in range(out_ref.shape[0]):
        for x in range(2):
            at = (2 * i + x) * BLOCK
            rows = dot(pick, both[:, at : at + BLOCK]).astype(BF16)
            for head in range(2):
                out_ref[i, (2 * head + x) * 16 : (2 * head + x) * 16 + 16] = rows[head * 16 : head * 16 + 16]
        out_ref[i, 64:] = hidden_ref[...]


def pack(core, key_rows, value_rows, hidden):
    steps = 2
    each = 8 // steps
    return pl.pallas_call(
        pack_kernel,
        grid=(steps,),
        in_specs=[
            pl.BlockSpec(memory_space=pltpu.SMEM),
            pl.BlockSpec((32, 2 * each * BLOCK), lambda i: (0, i)),
            pl.BlockSpec((32, 2 * each * BLOCK), lambda i: (0, i)),
            pl.BlockSpec((RESP, BLOCK), lambda i: (0, 0)),
        ],
        out_specs=pl.BlockSpec((each, PACKED, BLOCK), lambda i: (i, 0, 0)),
        out_shape=jax.ShapeDtypeStruct((8, PACKED, BLOCK), BF16),
        compiler_params=params(),
        name="pack",
    )(core, key_rows, value_rows, hidden)


def scale_kernel(info_ref, prompt_ref, resp_ref, gain_ref, out_ref, high, low):
    gain = gain_ref[info_ref[T_AT]]

    def put(at, count, values):
        values = values.astype(F32)
        out_ref[at : at + count] = (values * gain).astype(BF16)
        square = values * values
        top = square.astype(BF16)
        high[at : at + count] = top
        low[at : at + count] = (square - top.astype(F32)).astype(BF16)

    for half in range(2):
        put(ROWS * half, 128, prompt_ref[128 * half : 128 * half + 128])
        put(ROWS * half + 128, 32, resp_ref[32 * half : 32 * half + 32])
    high[320:448] = jnp.zeros((128, BLOCK), BF16)
    low[320:448] = jnp.zeros((128, BLOCK), BF16)
    ones = jnp.ones((16, BLOCK), BF16)
    row = iota((16, 128), 0)
    rows = jnp.zeros((16, 128), F32)
    for n, at in enumerate((0, 128, ROWS, ROWS + 128)):
        total = dot_t(ones, high[at : at + 128]) + dot_t(ones, low[at : at + 128])
        top = total.astype(BF16).astype(F32)
        rows = jnp.where(row == 2 * n, top, jnp.where(row == 2 * n + 1, total - top, rows))
    out_ref[320:, :128] = rows.astype(BF16)
    out_ref[320:, 128:] = jnp.zeros((16, BLOCK - 128), BF16)


def scale_rows(info, prompt, resp, gain):
    vmem = pl.BlockSpec(memory_space=pltpu.VMEM)
    return pl.pallas_call(
        scale_kernel,
        in_specs=[pl.BlockSpec(memory_space=pltpu.SMEM), vmem, vmem, vmem],
        out_shape=jax.ShapeDtypeStruct((2 * ROWS + 16, BLOCK), BF16),
        scratch_shapes=[pltpu.VMEM((448, BLOCK), BF16), pltpu.VMEM((448, BLOCK), BF16)],
        compiler_params=params(SMALL),
        name="scale_rows",
    )(info, prompt, resp, gain)


def partial_kernel(scalars_ref, weight_ref, own_ref, other_ref, *refs):
    out_ref = refs[-1]
    is_first = scalars_ref[1] == 0
    own, other = own_ref[: 2 * ROWS], other_ref[: 2 * ROWS]
    rows = (jnp.where(is_first, own, other), jnp.where(is_first, other, own))
    total = jnp.zeros((2 * ROWS, 256), F32)
    for x in range(2):
        weights = [weight_ref[:, (2 * head + x) * 16 : (2 * head + x) * 16 + 16] for head in range(2)]
        weights = [piece.reshape(128, BLOCK) for piece in weights]
        total += dot_t(rows[x], jnp.concatenate(weights, axis=0))
    total = total.astype(BF16)
    own_sums, other_sums = own_ref[2 * ROWS :, :128], other_ref[2 * ROWS :, :128]
    for head in range(2):
        for half in range(2):
            to = 2 * head + half
            out_ref[to, :ROWS] = total[ROWS * half : ROWS * half + ROWS, head * 128 : head * 128 + 128]
            sums = jnp.concatenate(
                [own_sums[4 * half : 4 * half + 4], other_sums[4 * half : 4 * half + 4], jnp.zeros((8, 128), BF16)],
                axis=0,
            )
            out_ref[to, ROWS:] = sums


def split_kernel(got_ref, *refs):
    weights_ref, hidden_ref = refs[-2:]
    weights_ref[...] = got_ref[:, :64]
    hidden_ref[...] = got_ref[:, 64:]


def split(got, after):
    return pl.pallas_call(
        split_kernel,
        in_specs=[pl.BlockSpec(memory_space=pltpu.VMEM)] * (1 + len(after)),
        out_shape=(jax.ShapeDtypeStruct((8, 64, BLOCK), BF16), jax.ShapeDtypeStruct((8, RESP, BLOCK), BF16)),
        compiler_params=params(SMALL),
        name="split",
    )(got, *after)


def partial_products(scalars, weights, own, other, before=None, after=None):
    def whole(shape):
        return pl.BlockSpec(shape, lambda i, scalars: (0,) * len(shape))

    rows = (2 * ROWS + 16, BLOCK)
    in_specs = [whole((8, 64, BLOCK)), whole(rows), whole(rows)]
    operands = [scalars, weights, own, other]
    aliases = {}
    if before is not None:
        in_specs.append(pl.BlockSpec(memory_space=pl.ANY))
        operands.append(before)
        aliases = {len(operands) - 1: 0}
    if after is not None:
        in_specs.append(pl.BlockSpec((16, 128), lambda i, scalars: (0, 0)))
        operands.append(after)
    return pl.pallas_call(
        partial_kernel,
        grid_spec=pltpu.PrefetchScalarGridSpec(
            num_scalar_prefetch=1,
            grid=(1,),
            in_specs=in_specs,
            out_specs=pl.BlockSpec((4, SENT_ROWS, 128), lambda i, scalars: (scalars[0], 0, 0)),
        ),
        out_shape=jax.ShapeDtypeStruct((8, SENT_ROWS, 128), BF16),
        input_output_aliases=aliases,
        compiler_params=params(SMALL),
        name="partial_products",
    )(*operands)


def turn(values, cosine, sine):
    return values * cosine + pltpu.roll(values, HALF, 1) * sine


def finish_kernel(parts_ref, trig_ref, *refs):
    out_ref = refs[-1]
    total = jnp.sum(parts_ref[...].astype(F32), axis=0)
    sums = total[ROWS:]
    column = []
    for n, count in enumerate((128, ROWS - 128)):
        line = sums[2 * n : 2 * n + 1] + sums[2 * n + 1 : 2 * n + 2] + sums[2 * n + 4 : 2 * n + 5]
        line += sums[2 * n + 5 : 2 * n + 6]
        diagonal = iota((count, 128), 0) == iota((count, 128), 1)
        spread = jnp.where(diagonal, jnp.broadcast_to(line, (count, 128)), 0.0)
        column.append(jnp.sum(spread, axis=1, keepdims=True))
    factor = lax.rsqrt(jnp.concatenate(column, axis=0) * (1.0 / D) + EPSILON)
    raw = (total[:ROWS] * factor).astype(BF16)
    row, col = iota((128, 128), 0), iota((128, 128), 1)
    target = ((row >> 3) & 1) * 64 + (row >> 4) * 8 + (row & 7)
    ordered = dot(raw, jnp.where(col == target, 1.0, 0.0).astype(BF16))
    beside = dot(raw, jnp.where(col == (target ^ 32), 1.0, 0.0).astype(BF16))
    result = (ordered * trig_ref[0, :ROWS] + beside * trig_ref[1, :ROWS]).astype(BF16)
    for i in range(out_ref.shape[0]):
        out_ref[i] = result


def finish_keys(parts, trig, *after):
    return pl.pallas_call(
        finish_kernel,
        in_specs=[pl.BlockSpec(memory_space=pltpu.VMEM)] * (2 + len(after)),
        out_shape=jax.ShapeDtypeStruct((16, ROWS, 128), BF16),
        compiler_params=params(SMALL),
        cost_estimate=LONG,
        name="finish_keys",
    )(parts, trig, *after)


def by_xl(natural):
    return ((natural >> 3) & 1) * 64 + (natural >> 4) * 8 + (natural & 7)


def query_kernel(info_ref, gain_ref, trig_ref, weight_ref, own_ref, other_ref, out_ref):
    xl = info_ref[XL_AT]
    total = jnp.zeros((RESP, 256), F32)
    squares = jnp.zeros((RESP, 1), F32)
    for z in range(8):
        for j, ref in enumerate((own_ref, other_ref)):
            x = j ^ xl
            hidden = ref[z].astype(F32)
            scaled = (hidden * gain_ref[2 * z + x]).astype(BF16)
            total += dot(scaled, weight_ref[pl.ds(pl.multiple_of((2 * z + x) * BLOCK, BLOCK), BLOCK)])
            squares += jnp.sum(hidden * hidden, axis=1, keepdims=True)
    factor = lax.rsqrt(squares * (1.0 / D) + EPSILON)
    row, col = iota((128, 128), 0), iota((128, 128), 1)
    order = jnp.where(col == by_xl(row), 1.0, 0.0).astype(BF16)
    for h in range(2):
        part = slice(h * HEAD_DIM, (h + 1) * HEAD_DIM)
        query = turn(total[:, part] * factor, trig_ref[0, ROWS:], trig_ref[1, ROWS:])
        out_ref[:, part] = dot(query.astype(BF16), order).astype(BF16)


def queries_of(info, gain, weight, trig, own, other):
    vmem = pl.BlockSpec(memory_space=pltpu.VMEM)
    return pl.pallas_call(
        query_kernel,
        in_specs=[pl.BlockSpec(memory_space=pltpu.SMEM)] + [vmem] * 5,
        out_shape=jax.ShapeDtypeStruct((RESP, 256), BF16),
        compiler_params=params(SMALL),
        cost_estimate=LONG,
        name="queries",
    )(info, gain, trig, weight, own, other)


def attend_kernel(info_ref, rows_ref, *refs):
    queries, outs = refs[:4], refs[4:]
    own_y = info_ref[Y_AT]

    def joined(block, at, count):
        first, second = rows_ref[block, pl.ds(at, count)], rows_ref[block + 1, pl.ds(at, count)]
        keys = jnp.concatenate([first[:, :HALF], second[:, :HALF]], axis=1)
        return keys, jnp.concatenate([first[:, HALF:], second[:, HALF:]], axis=1)

    prompt = [joined(2 * i, 0, 128) for i in range(8)]
    prompt_keys, prompt_values = (jnp.concatenate([p[n] for p in prompt], axis=0) for n in range(2))
    place = info_ref[PLACE_AT] * 4
    own = [joined(place + 2 * half, 128, 32) for half in range(2)]
    own_keys, own_values = (jnp.concatenate([o[n] for o in own], axis=0) for n in range(2))
    scale = HEAD_DIM ** (-0.5)
    power = scale * math.log2(math.e)

    column = iota((1, 1024), 1)
    sample = (column >> 9) * 8 + own_y * 2 + ((column >> 8) & 1)
    live = sample * PROMPT_ROWS + (column & 255) < info_ref[LENGTH_AT]
    causal = iota((2 * RESP, RESP), 1) <= (iota((2 * RESP, RESP), 0) & (RESP - 1))
    lane = iota((RESP, 128), 1)

    for i in range(4):
        query = jnp.concatenate([queries[i][:, :HEAD_DIM], queries[i][:, HEAD_DIM:]], axis=0)
        far = jnp.where(live, dot_t(query, prompt_keys), NEG_BIG)
        top = jnp.max(far, axis=1, keepdims=True)
        if i == 0:
            near = jnp.where(causal, dot_t(query, own_keys), NEG_BIG)
            top = jnp.maximum(top, jnp.max(near, axis=1, keepdims=True))
        top = jnp.maximum(top, 0.5 * NEG_BIG)
        far = jnp.exp2((far - top) * power)
        total = jnp.sum(far, axis=1, keepdims=True)
        summed = dot(far.astype(BF16), prompt_values)
        if i == 0:
            near = jnp.exp2((near - top) * power)
            total += jnp.sum(near, axis=1, keepdims=True)
            summed += dot(near.astype(BF16), own_values)
        some = total > 0.0
        safe = jnp.where(some, total, 1.0)
        result = (summed / safe).astype(BF16)
        level = jnp.where(some, top * scale + jnp.log(safe), NEG_BIG)
        first = level.astype(BF16).astype(F32)
        rest = level - first
        second = rest.astype(BF16).astype(F32)
        third = rest - second
        extra = jnp.zeros((RESP, 128), F32)
        for h in range(2):
            mine = slice(h * RESP, (h + 1) * RESP)
            outs[i][:, h * HEAD_DIM : (h + 1) * HEAD_DIM] = result[mine]
            for n, piece in enumerate((first, second, third)):
                extra = jnp.where(lane == 3 * h + n, piece[mine], extra)
        outs[i][:, 256:] = extra.astype(BF16)


def attend(info, rows, queries):
    vmem = pl.BlockSpec(memory_space=pltpu.VMEM)
    return pl.pallas_call(
        attend_kernel,
        in_specs=[pl.BlockSpec(memory_space=pltpu.SMEM)] + [vmem] * 5,
        out_shape=(jax.ShapeDtypeStruct((RESP, 384), BF16),) * 4,
        compiler_params=params(SMALL),
        name="attend",
    )(info, rows, *queries)


def merge_kernel(*refs):
    parts, out_ref = refs[:4], refs[4]
    lane = iota((RESP, 128), 1)
    row, col = iota((128, 128), 0), iota((128, 128), 1)
    order = jnp.where(row == by_xl(col), 1.0, 0.0).astype(BF16)
    extras = [part[:, 256:].astype(F32) for part in parts]
    for h in range(2):
        head = slice(h * HEAD_DIM, (h + 1) * HEAD_DIM)
        mine = jnp.logical_and(lane >= 3 * h, lane < 3 * h + 3)
        levels = [jnp.sum(jnp.where(mine, e, 0.0), axis=1, keepdims=True) for e in extras]
        top = functools.reduce(jnp.maximum, levels)
        shares = [jnp.exp(level - top) for level in levels]
        total = functools.reduce(jnp.add, shares)
        pieces = [share * part[:, head].astype(F32) for share, part in zip(shares, parts)]
        mean = (functools.reduce(jnp.add, pieces) / total).astype(BF16)
        out_ref[:, head] = dot(mean, order).astype(BF16)


def merge(parts):
    vmem = pl.BlockSpec(memory_space=pltpu.VMEM)
    return pl.pallas_call(
        merge_kernel,
        in_specs=[vmem] * 4,
        out_shape=jax.ShapeDtypeStruct((RESP, 256), BF16),
        compiler_params=params(SMALL),
        name="merge",
    )(*parts)


def z_of(i, info):
    return (4 * info[CORE_AT] + 2 * (info[Y_AT] % 2)) ^ i


def project_own_kernel(own_ref, *refs):
    weights, out_ref = refs[:4], refs[4]
    for i in range(8):
        out_ref[i] = dot(own_ref[...], weights[i // 2][:, pl.ds((i % 2) * BLOCK, BLOCK)])


def project_own(own, weights):
    vmem = pl.BlockSpec(memory_space=pltpu.VMEM)
    return pl.pallas_call(
        project_own_kernel,
        in_specs=[vmem] * 5,
        out_shape=jax.ShapeDtypeStruct((8, RESP, BLOCK), F32),
        compiler_params=params(SMALL),
        cost_estimate=LONG,
        name="project_own",
    )(own, *weights)


def project_kernel(info_ref, started_ref, other_ref, *refs):
    cross, out_ref = refs[:4], refs[4]
    for i in range(8):
        result = started_ref[i] + dot(other_ref[...], cross[i // 2][:, pl.ds((i % 2) * BLOCK, BLOCK)])
        out_ref[z_of(i, info_ref)] = result.astype(BF16)


def project(info, started, other, cross):
    vmem = pl.BlockSpec(memory_space=pltpu.VMEM)
    return pl.pallas_call(
        project_kernel,
        in_specs=[pl.BlockSpec(memory_space=pltpu.SMEM)] + [vmem] * 6,
        out_shape=jax.ShapeDtypeStruct((8, RESP, BLOCK), BF16),
        compiler_params=params(SMALL),
        name="project",
    )(info, started, other, *cross)


def pick_kernel(info_ref, weight_ref, *refs):
    own_refs, sent_ref = refs[:4], refs[4]

    def columns(i, x):
        at = (2 * z_of(i, info_ref) + x) * BLOCK
        return weight_ref[:, pl.ds(pl.multiple_of(at, BLOCK), BLOCK)]

    xl = info_ref[XL_AT]
    for i in range(8):
        own_refs[i // 2][:, (i % 2) * BLOCK : (i % 2) * BLOCK + BLOCK] = columns(i, xl)
    for i in range(2):
        sent_ref[:, i * BLOCK : (i + 1) * BLOCK] = columns(i, 1 - xl)


def pick_columns(info, weight):
    return pl.pallas_call(
        pick_kernel,
        in_specs=[pl.BlockSpec(memory_space=pltpu.SMEM), pl.BlockSpec(memory_space=pltpu.VMEM)],
        out_shape=(jax.ShapeDtypeStruct((256, 2 * BLOCK), BF16),) * 5,
        compiler_params=params(SMALL),
        name="pick_columns",
    )(info, weight)


def swap(values, axis):
    return lax.all_to_all(values, axis, 0, 0, tiled=False)


def body(
    response_hidden,
    prompt_hidden,
    norm_gain,
    query_weight,
    key_weight,
    value_weight,
    output_weight,
    response_lengths,
    prompt_length,
):
    length = prompt_length[0]
    core, y = lax.axis_index("core"), lax.axis_index("y")
    sample, half, xl = lax.axis_index(SAMPLE), lax.axis_index("zl"), lax.axis_index("xl")
    gain = norm_gain.astype(F32).reshape(16, 1, BLOCK)

    row = jnp.arange(ROWS + RESP, dtype=jnp.int32)[:, None]
    positions = jnp.where(
        row < 128,
        sample * PROMPT_ROWS + half * 128 + row,
        jnp.where(row < ROWS, length + half * 32 + row - 128, length + row - ROWS),
    )
    lane = jnp.arange(HEAD_DIM, dtype=jnp.int32)[None, :]
    entry = ((lane >> 3) * 2 + xl) * 8 + (lane & 7)
    entry = jnp.where(row < ROWS, entry, lane)
    still = (row < ROWS) & (lane >= HALF)
    inverse = ROPE_BASE ** (-((entry % HALF).astype(F32) * 2.0 / HEAD_DIM))
    angles = jnp.where(still, 0.0, positions.astype(F32) * inverse)
    trig = jnp.stack([jnp.cos(angles), jnp.sin(angles) * jnp.where(entry < HALF, -1.0, 1.0)])

    info = jnp.stack(
        [core, xl, lax.axis_index(TENSOR), y, lax.axis_index(("xh", "core")), length]
    ).astype(jnp.int32)
    flip = [(0, 1), (1, 0)]

    packed = pack(core.reshape(1), key_weight.T, value_weight.T, response_hidden)
    got = swap(packed, ZRING)
    scaled = scale_rows(info, prompt_hidden, response_hidden, gain)
    beside = lax.ppermute(scaled, "xl", flip)
    *own, sent = pick_columns(info, output_weight)
    first = lax.ppermute(sent, "xl", flip)
    weights, own_hidden = split(got, (beside, sent))
    other_weights = lax.ppermute(weights, "core", flip)
    products = partial_products(jnp.stack([core, xl]), weights, scaled, beside)
    products = partial_products(jnp.stack([1 - core, xl]), other_weights, scaled, beside, products, first)
    products = swap(products, ZRING)
    other_hidden = lax.ppermute(own_hidden, "xl", flip)
    second = lax.ppermute(first, "y", [(i, i ^ 1) for i in range(4)])
    queries = queries_of(info, gain, query_weight, trig, own_hidden, other_hidden)
    cross = (first, second, lax.ppermute(first, "core", flip), lax.ppermute(second, "core", flip))
    rows = finish_keys(products, trig, queries, second)
    rows = swap(rows, KEY_GROUP)

    def along(values, step):
        return lax.ppermute(values, "y", [(i, (i + step) % 4) for i in range(4)])

    pooled = [queries] + [along(queries, step) for step in (1, 2, 3)]
    parts = attend(info, rows, pooled)
    attention = merge([parts[0]] + [along(parts[step], -step) for step in (1, 2, 3)])
    partner = lax.ppermute(attention, "xl", flip)
    partial = project(info, project_own(attention, own), partner, cross)
    summed = jnp.sum(swap(partial, ZRING).astype(F32), axis=0)
    live = jnp.arange(RESP, dtype=jnp.int32) < response_lengths[0]
    return jnp.where(live[:, None], summed, 0.0).astype(BF16)


def solution(mesh):
    names = tuple(name for name, _ in PARTS)
    sizes = tuple(size for _, size in PARTS)
    fine = Mesh(mesh.devices.reshape(sizes), names)
    return jax.shard_map(
        body,
        mesh=fine,
        in_specs=(
            P(SAMPLE, TENSOR),
            P(SAMPLE, TENSOR),
            P(),
            P(None, TENSOR),
            P(None, TENSOR),
            P(None, TENSOR),
            P(TENSOR, None),
            P(SAMPLE),
            P(),
        ),
        out_specs=P(SAMPLE, TENSOR),
        check_vma=False,
    )
```

```python
import functools
import math

import jax
import jax.numpy as jnp
from jax import lax
from jax.experimental import pallas as pl
from jax.experimental.pallas import tpu as pltpu
from jax.sharding import Mesh
from jax.sharding import PartitionSpec as P

PARTS = (("xh", 2), ("y", 4), ("core", 2), ("k", 4), ("zl", 2), ("xl", 2))
SAMPLE = ("xh", "y", "core")
TENSOR = ("k", "zl", "xl")
ZRING = ("k", "zl")
KEY_GROUP = ("xh", "core", "zl", "xl")

D = 8192
BLOCK = 512
HEAD_DIM = 128
HALF = 64
RESP = 64
PROMPT_ROWS = 256
ROWS = 160
SHARED_ROWS = 144
SENT_ROWS = ROWS + 16
PACKED = 64 + RESP
EPSILON = 1e-05
ROPE_BASE = 500000.0
NEG_BIG = -1e30
CORE_AT, XL_AT, T_AT, Y_AT, PLACE_AT, LENGTH_AT = 0, 1, 2, 3, 4, 5
F32 = jnp.float32
BF16 = jnp.bfloat16
SMALL = 12 * 1024 * 1024


def iota(shape, dim):
    return lax.broadcasted_iota(jnp.int32, shape, dim)


def dot_t(a, b):
    return lax.dot_general(a, b, (((1,), (1,)), ((), ())), preferred_element_type=F32)


def dot(a, b):
    return lax.dot_general(a, b, (((1,), (0,)), ((), ())), preferred_element_type=F32)


LONG = pl.CostEstimate(flops=30_000_000_000, bytes_accessed=1_000_000, transcendentals=0)


def params(limit=None):
    return pltpu.CompilerParams(vmem_limit_bytes=limit)


def pack_kernel(core_ref, key_ref, value_ref, hidden_ref, out_ref):
    row, col = iota((32, 64), 0), iota((32, 64), 1)
    source = ((row >> 2) & 1) * 32 + (4 * core_ref[0] + (row & 3)) * 4 + (row >> 3)
    pick = jnp.where(col == source, 1.0, 0.0).astype(BF16)
    both = jnp.concatenate([key_ref[...], value_ref[...]], axis=0)
    for i in range(out_ref.shape[0]):
        for x in range(2):
            at = (2 * i + x) * BLOCK
            out_ref[i, 32 * x : 32 * x + 32] = dot(pick, both[:, at : at + BLOCK]).astype(BF16)
        out_ref[i, 64:] = hidden_ref[...]


def pack(core, key_rows, value_rows, hidden):
    steps = 2
    each = 8 // steps
    return pl.pallas_call(
        pack_kernel,
        grid=(steps,),
        in_specs=[
            pl.BlockSpec(memory_space=pltpu.SMEM),
            pl.BlockSpec((32, 2 * each * BLOCK), lambda i: (0, i)),
            pl.BlockSpec((32, 2 * each * BLOCK), lambda i: (0, i)),
            pl.BlockSpec((RESP, BLOCK), lambda i: (0, 0)),
        ],
        out_specs=pl.BlockSpec((each, PACKED, BLOCK), lambda i: (i, 0, 0)),
        out_shape=jax.ShapeDtypeStruct((8, PACKED, BLOCK), BF16),
        compiler_params=params(),
        name="pack",
    )(core, key_rows, value_rows, hidden)


def scale_kernel(info_ref, prompt_ref, resp_ref, gain_ref, out_ref, high, low):
    gain = gain_ref[info_ref[T_AT]]

    def put(at, count, values):
        values = values.astype(F32)
        out_ref[at : at + count] = (values * gain).astype(BF16)
        square = values * values
        top = square.astype(BF16)
        high[at : at + count] = top
        low[at : at + count] = (square - top.astype(F32)).astype(BF16)

    for half in range(2):
        put(ROWS * half, 128, prompt_ref[128 * half : 128 * half + 128])
        put(ROWS * half + 128, 32, resp_ref[32 * half : 32 * half + 32])
    high[320:448] = jnp.zeros((128, BLOCK), BF16)
    low[320:448] = jnp.zeros((128, BLOCK), BF16)
    ones = jnp.ones((16, BLOCK), BF16)
    row = iota((16, 128), 0)
    rows = jnp.zeros((16, 128), F32)
    for n, at in enumerate((0, 128, ROWS, ROWS + 128)):
        total = dot_t(ones, high[at : at + 128]) + dot_t(ones, low[at : at + 128])
        top = total.astype(BF16).astype(F32)
        rows = jnp.where(row == 2 * n, top, jnp.where(row == 2 * n + 1, total - top, rows))
    out_ref[320:, :128] = rows.astype(BF16)
    out_ref[320:, 128:] = jnp.zeros((16, BLOCK - 128), BF16)


def scale_rows(info, prompt, resp, gain):
    vmem = pl.BlockSpec(memory_space=pltpu.VMEM)
    return pl.pallas_call(
        scale_kernel,
        in_specs=[pl.BlockSpec(memory_space=pltpu.SMEM), vmem, vmem, vmem],
        out_shape=jax.ShapeDtypeStruct((2 * ROWS + 16, BLOCK), BF16),
        scratch_shapes=[pltpu.VMEM((448, BLOCK), BF16), pltpu.VMEM((448, BLOCK), BF16)],
        compiler_params=params(SMALL),
        name="scale_rows",
    )(info, prompt, resp, gain)


def split_kernel(got_ref, *refs):
    refs[-1][...] = got_ref[:, 64:]


def split(got, after):
    return pl.pallas_call(
        split_kernel,
        in_specs=[pl.BlockSpec(memory_space=pltpu.VMEM)] * (1 + len(after)),
        out_shape=jax.ShapeDtypeStruct((8, RESP, BLOCK), BF16),
        compiler_params=params(SMALL),
        name="split",
    )(got, *after)


def partial_kernel(info_ref, got_ref, *refs):
    out_ref = refs[4]
    xl, core = info_ref[XL_AT], info_ref[CORE_AT]
    weights = [got_ref[:, pl.ds(pl.multiple_of(32 * x, 32), 32)].reshape(256, BLOCK) for x in (xl, 1 - xl)]
    row, col = iota((256, 512), 0), iota((256, 512), 1)
    target = ((row >> 3) & 3) * 128 + (row >> 5) * 8 + (row & 7)
    total = jnp.zeros((2 * ROWS, 512), F32)
    sums = []
    for n, at in enumerate((core, 1 - core)):
        here, there = refs[2 * n], refs[2 * n + 1]
        raw = dot_t(here[: 2 * ROWS], weights[0]) + dot_t(there[: 2 * ROWS], weights[1])
        pick = jnp.where(col == target + 64 * at, 1.0, 0.0).astype(BF16)
        total += dot(raw.astype(BF16), pick)
        sums.append((here[2 * ROWS :, :128], there[2 * ROWS :, :128]))
    total = total.astype(BF16)
    for half in range(2):
        lines = [[piece[4 * half : 4 * half + 4] for piece in pair] for pair in sums]
        lines = [jnp.concatenate(lines[0] + lines[1], axis=0), jnp.concatenate(lines[1] + lines[0], axis=0)]
        for head in range(4):
            to = 2 * head + half
            out_ref[to, :ROWS] = total[ROWS * half : ROWS * half + ROWS, head * 128 : head * 128 + 128]
            out_ref[to, ROWS:] = jnp.where(core == 0, lines[0], lines[1])


def partial_products(info, got, blocks):
    vmem = pl.BlockSpec(memory_space=pltpu.VMEM)
    return pl.pallas_call(
        partial_kernel,
        in_specs=[pl.BlockSpec(memory_space=pltpu.SMEM)] + [vmem] * 5,
        out_shape=jax.ShapeDtypeStruct((8, SENT_ROWS, 128), BF16),
        compiler_params=params(SMALL),
        name="partial_products",
    )(info, got, *blocks)


def turn(values, cosine, sine):
    return values * cosine + pltpu.roll(values, HALF, 1) * sine


def finish_kernel(parts_ref, trig_ref, *refs):
    out_ref = refs[-1]
    total = jnp.sum(parts_ref[...].astype(F32), axis=0)
    sums = total[ROWS:]
    factors = []
    for core in range(2):
        column = []
        for n, count in enumerate((128, ROWS - 128)):
            at = 8 * core + 2 * n
            line = sums[at : at + 1] + sums[at + 1 : at + 2] + sums[at + 4 : at + 5] + sums[at + 5 : at + 6]
            diagonal = iota((count, 128), 0) == iota((count, 128), 1)
            spread = jnp.where(diagonal, jnp.broadcast_to(line, (count, 128)), 0.0)
            column.append(jnp.sum(spread, axis=1, keepdims=True))
        factors.append(lax.rsqrt(jnp.concatenate(column, axis=0) * (1.0 / D) + EPSILON))
    factor = jnp.where(iota((ROWS, 128), 1) < 64, factors[0], factors[1])
    raw = (total[:ROWS] * factor).astype(BF16)
    row, col = iota((128, 128), 0), iota((128, 128), 1)
    target = (row & 64) + ((row >> 2) & 1) * 32 + ((row >> 3) & 7) * 4 + (row & 3)
    ordered = dot(raw, jnp.where(col == target, 1.0, 0.0).astype(BF16))
    beside = dot(raw, jnp.where(col == (target ^ 16), 1.0, 0.0).astype(BF16))
    result = ordered * trig_ref[0, :ROWS] + beside * trig_ref[1, :ROWS]
    prompt = result[:128].astype(BF16)
    first, second = result[128:144], result[144:160]
    left = iota((16, 128), 1) < 64
    resp = (
        jnp.where(left, first, pltpu.roll(second, 64, 1)).astype(BF16),
        jnp.where(left, pltpu.roll(first, 64, 1), second).astype(BF16),
    )
    for i in range(out_ref.shape[0]):
        out_ref[i, :128] = prompt
        out_ref[i, 128:] = resp[(i >> 2) & 1]


def finish_keys(parts, trig, *after):
    return pl.pallas_call(
        finish_kernel,
        in_specs=[pl.BlockSpec(memory_space=pltpu.VMEM)] * (2 + len(after)),
        out_shape=jax.ShapeDtypeStruct((16, SHARED_ROWS, 128), BF16),
        compiler_params=params(SMALL),
        cost_estimate=LONG,
        name="finish_keys",
    )(parts, trig, *after)


def by_device(natural):
    return ((natural >> 3) & 1) * 64 + ((natural >> 2) & 1) * 32 + (natural >> 4) * 4 + (natural & 3)


def query_kernel(info_ref, gain_ref, trig_ref, weight_ref, own_ref, other_ref, out_ref):
    xl = info_ref[XL_AT]
    total = jnp.zeros((RESP, 256), F32)
    squares = jnp.zeros((RESP, 1), F32)
    for z in range(8):
        for j, ref in enumerate((own_ref, other_ref)):
            x = j ^ xl
            hidden = ref[z].astype(F32)
            scaled = (hidden * gain_ref[2 * z + x]).astype(BF16)
            total += dot(scaled, weight_ref[pl.ds(pl.multiple_of((2 * z + x) * BLOCK, BLOCK), BLOCK)])
            squares += jnp.sum(hidden * hidden, axis=1, keepdims=True)
    factor = lax.rsqrt(squares * (1.0 / D) + EPSILON)
    row, col = iota((128, 128), 0), iota((128, 128), 1)
    order = jnp.where(col == by_device(row), 1.0, 0.0).astype(BF16)
    for h in range(2):
        part = slice(h * HEAD_DIM, (h + 1) * HEAD_DIM)
        query = turn(total[:, part] * factor, trig_ref[0, ROWS:], trig_ref[1, ROWS:])
        out_ref[:, part] = dot(query.astype(BF16), order).astype(BF16)


def queries_of(info, gain, weight, trig, own, other):
    vmem = pl.BlockSpec(memory_space=pltpu.VMEM)
    return pl.pallas_call(
        query_kernel,
        in_specs=[pl.BlockSpec(memory_space=pltpu.SMEM)] + [vmem] * 5,
        out_shape=jax.ShapeDtypeStruct((RESP, 256), BF16),
        compiler_params=params(SMALL),
        cost_estimate=LONG,
        name="queries",
    )(info, gain, trig, weight, own, other)


def attend_kernel(info_ref, rows_ref, *refs):
    queries, outs = refs[:4], refs[4:]
    own_y = info_ref[Y_AT]

    row, col = iota((512, 512), 0), iota((512, 512), 1)
    target = ((row >> 5) & 3) * 128 + ((row >> 7) & 1) * 64 + (row >> 8) * 32 + (row & 31)
    pick = jnp.where(col == target, 1.0, 0.0).astype(BF16)

    def joined(xh, zl, at, count):
        pieces = [rows_ref[xh * 8 + core * 4 + zl * 2 + x, at : at + count] for core in range(2) for x in range(2)]
        return dot(jnp.concatenate(pieces, axis=1), pick).astype(BF16)

    prompt = [[joined(xh, zl, 0, 128) for zl in range(2)] for xh in range(2)]

    def prompt_rows(kv):
        return jnp.concatenate(
            [
                prompt[xh][zl][:, (2 * core + kv) * 128 : (2 * core + kv) * 128 + 128]
                for xh in range(2)
                for core in range(2)
                for zl in range(2)
            ],
            axis=0,
        )

    prompt_keys, prompt_values = prompt_rows(0), prompt_rows(1)
    own_xh = info_ref[PLACE_AT] // 2
    own = [joined(own_xh, zl, 128, 16) for zl in range(2)]

    def own_rows(kv):
        return jnp.concatenate(
            [o[:, (2 * n + kv) * 128 : (2 * n + kv) * 128 + 128] for o in own for n in range(2)], axis=0
        )

    own_keys, own_values = own_rows(0), own_rows(1)
    scale = HEAD_DIM ** (-0.5)
    power = scale * math.log2(math.e)

    column = iota((1, 1024), 1)
    sample = (column >> 9) * 8 + own_y * 2 + ((column >> 8) & 1)
    live = sample * PROMPT_ROWS + (column & 255) < info_ref[LENGTH_AT]
    causal = iota((2 * RESP, RESP), 1) <= (iota((2 * RESP, RESP), 0) & (RESP - 1))
    lane = iota((RESP, 128), 1)

    for i in range(4):
        query = jnp.concatenate([queries[i][:, :HEAD_DIM], queries[i][:, HEAD_DIM:]], axis=0)
        far = jnp.where(live, dot_t(query, prompt_keys), NEG_BIG)
        top = jnp.max(far, axis=1, keepdims=True)
        if i == 0:
            near = jnp.where(causal, dot_t(query, own_keys), NEG_BIG)
            top = jnp.maximum(top, jnp.max(near, axis=1, keepdims=True))
        top = jnp.maximum(top, 0.5 * NEG_BIG)
        far = jnp.exp2((far - top) * power)
        total = jnp.sum(far, axis=1, keepdims=True)
        summed = dot(far.astype(BF16), prompt_values)
        if i == 0:
            near = jnp.exp2((near - top) * power)
            total += jnp.sum(near, axis=1, keepdims=True)
            summed += dot(near.astype(BF16), own_values)
        some = total > 0.0
        safe = jnp.where(some, total, 1.0)
        result = (summed / safe).astype(BF16)
        level = jnp.where(some, top * scale + jnp.log(safe), NEG_BIG)
        first = level.astype(BF16).astype(F32)
        rest = level - first
        second = rest.astype(BF16).astype(F32)
        third = rest - second
        extra = jnp.zeros((RESP, 128), F32)
        for h in range(2):
            mine = slice(h * RESP, (h + 1) * RESP)
            outs[i][:, h * HEAD_DIM : (h + 1) * HEAD_DIM] = result[mine]
            for n, piece in enumerate((first, second, third)):
                extra = jnp.where(lane == 3 * h + n, piece[mine], extra)
        outs[i][:, 256:] = extra.astype(BF16)


def attend(info, rows, queries):
    vmem = pl.BlockSpec(memory_space=pltpu.VMEM)
    return pl.pallas_call(
        attend_kernel,
        in_specs=[pl.BlockSpec(memory_space=pltpu.SMEM)] + [vmem] * 5,
        out_shape=(jax.ShapeDtypeStruct((RESP, 384), BF16),) * 4,
        compiler_params=params(SMALL),
        name="attend",
    )(info, rows, *queries)


def merge_kernel(*refs):
    parts, out_ref = refs[:4], refs[4]
    lane = iota((RESP, 128), 1)
    row, col = iota((128, 128), 0), iota((128, 128), 1)
    order = jnp.where(row == by_device(col), 1.0, 0.0).astype(BF16)
    extras = [part[:, 256:].astype(F32) for part in parts]
    for h in range(2):
        head = slice(h * HEAD_DIM, (h + 1) * HEAD_DIM)
        mine = jnp.logical_and(lane >= 3 * h, lane < 3 * h + 3)
        levels = [jnp.sum(jnp.where(mine, e, 0.0), axis=1, keepdims=True) for e in extras]
        top = functools.reduce(jnp.maximum, levels)
        shares = [jnp.exp(level - top) for level in levels]
        total = functools.reduce(jnp.add, shares)
        pieces = [share * part[:, head].astype(F32) for share, part in zip(shares, parts)]
        mean = (functools.reduce(jnp.add, pieces) / total).astype(BF16)
        out_ref[:, head] = dot(mean, order).astype(BF16)


def merge(parts):
    vmem = pl.BlockSpec(memory_space=pltpu.VMEM)
    return pl.pallas_call(
        merge_kernel,
        in_specs=[vmem] * 4,
        out_shape=jax.ShapeDtypeStruct((RESP, 256), BF16),
        compiler_params=params(SMALL),
        name="merge",
    )(*parts)


def z_of(i, info):
    return (4 * info[CORE_AT]) ^ i


def project_own_kernel(info_ref, own_ref, weight_ref, out_ref):
    for i in range(8):
        at = (2 * z_of(i, info_ref) + info_ref[XL_AT]) * BLOCK
        out_ref[i] = dot(own_ref[...], weight_ref[:, pl.ds(pl.multiple_of(at, BLOCK), BLOCK)])


def project_own(info, own, weight):
    vmem = pl.BlockSpec(memory_space=pltpu.VMEM)
    return pl.pallas_call(
        project_own_kernel,
        in_specs=[pl.BlockSpec(memory_space=pltpu.SMEM)] + [vmem] * 2,
        out_shape=jax.ShapeDtypeStruct((8, RESP, BLOCK), F32),
        compiler_params=params(SMALL),
        cost_estimate=LONG,
        name="project_own",
    )(info, own, weight)


def project_kernel(info_ref, started_ref, other_ref, *refs):
    cross, out_ref = refs[:4], refs[4]
    for i in range(8):
        result = started_ref[i] + dot(other_ref[...], cross[i // 2][:, pl.ds((i % 2) * BLOCK, BLOCK)])
        out_ref[z_of(i, info_ref)] = result.astype(BF16)


def project(info, started, other, cross):
    vmem = pl.BlockSpec(memory_space=pltpu.VMEM)
    return pl.pallas_call(
        project_kernel,
        in_specs=[pl.BlockSpec(memory_space=pltpu.SMEM)] + [vmem] * 6,
        out_shape=jax.ShapeDtypeStruct((8, RESP, BLOCK), BF16),
        compiler_params=params(SMALL),
        name="project",
    )(info, started, other, *cross)


def pick_kernel(info_ref, weight_ref, after_ref, *out_refs):
    for i in range(4):
        at = (2 * z_of(i, info_ref) + 1 - info_ref[XL_AT]) * BLOCK
        columns = weight_ref[:, pl.ds(pl.multiple_of(at, BLOCK), BLOCK)]
        out_refs[i // 2][:, (i % 2) * BLOCK : (i % 2) * BLOCK + BLOCK] = columns


def pick_columns(info, weight, after):
    vmem = pl.BlockSpec(memory_space=pltpu.VMEM)
    return pl.pallas_call(
        pick_kernel,
        in_specs=[pl.BlockSpec(memory_space=pltpu.SMEM)] + [vmem] * 2,
        out_shape=(jax.ShapeDtypeStruct((256, 2 * BLOCK), BF16),) * 2,
        compiler_params=params(SMALL),
        name="pick_columns",
    )(info, weight, after)


def swap(values, axis):
    return lax.all_to_all(values, axis, 0, 0, tiled=False)


def body(
    response_hidden,
    prompt_hidden,
    norm_gain,
    query_weight,
    key_weight,
    value_weight,
    output_weight,
    response_lengths,
    prompt_length,
):
    length = prompt_length[0]
    core, y = lax.axis_index("core"), lax.axis_index("y")
    sample, half, xl = lax.axis_index(SAMPLE), lax.axis_index("zl"), lax.axis_index("xl")
    gain = norm_gain.astype(F32).reshape(16, 1, BLOCK)

    row = jnp.arange(ROWS + RESP, dtype=jnp.int32)[:, None]
    lane = jnp.arange(HEAD_DIM, dtype=jnp.int32)[None, :]
    sample_of = sample - core + (lane >> 6)
    positions = jnp.where(
        row < 128,
        sample_of * PROMPT_ROWS + half * 128 + row,
        jnp.where(row < ROWS, length + half * 32 + row - 128, length + row - ROWS),
    )
    entry = (2 * ((lane >> 2) & 7) + xl) * 8 + 4 * core + (lane & 3)
    entry = jnp.where(row < ROWS, entry, lane)
    still = (row < ROWS) & ((lane & 32) > 0)
    inverse = ROPE_BASE ** (-((entry % HALF).astype(F32) * 2.0 / HEAD_DIM))
    angles = jnp.where(still, 0.0, positions.astype(F32) * inverse)
    trig = jnp.stack([jnp.cos(angles), jnp.sin(angles) * jnp.where(entry < HALF, -1.0, 1.0)])

    info = jnp.stack(
        [core, xl, lax.axis_index(TENSOR), y, lax.axis_index(("xh", "core")), length]
    ).astype(jnp.int32)
    flip = [(0, 1), (1, 0)]

    packed = pack(core.reshape(1), key_weight.T, value_weight.T, response_hidden)
    got = swap(packed, ZRING)
    scaled = scale_rows(info, prompt_hidden, response_hidden, gain)
    beside = lax.ppermute(scaled, "xl", flip)
    crossed = lax.ppermute(scaled, "core", flip), lax.ppermute(beside, "core", flip)
    sent = pick_columns(info, output_weight, scaled)
    early, late = (lax.ppermute(piece, "xl", flip) for piece in sent)
    own_hidden = split(got, (*crossed, early, sent[1], trig))
    other_hidden = lax.ppermute(own_hidden, "xl", flip)
    products = partial_products(info, got, (scaled, beside, *crossed))
    products = swap(products, ZRING)
    queries = queries_of(info, gain, query_weight, trig, own_hidden, other_hidden)
    cross = (early, late, lax.ppermute(early, "core", flip), lax.ppermute(late, "core", flip))
    rows = finish_keys(products, trig, queries)
    rows = swap(rows, KEY_GROUP)

    def along(values, step):
        return lax.ppermute(values, "y", [(i, (i + step) % 4) for i in range(4)])

    pooled = [queries] + [along(queries, step) for step in (1, 2, 3)]
    parts = attend(info, rows, pooled)
    attention = merge([parts[0]] + [along(parts[step], -step) for step in (1, 2, 3)])
    partner = lax.ppermute(attention, "xl", flip)
    partial = project(info, project_own(info, attention, output_weight), partner, cross)
    summed = jnp.sum(swap(partial, ZRING).astype(F32), axis=0)
    live = jnp.arange(RESP, dtype=jnp.int32) < response_lengths[0]
    return jnp.where(live[:, None], summed, 0.0).astype(BF16)


def solution(mesh):
    names = tuple(name for name, _ in PARTS)
    sizes = tuple(size for _, size in PARTS)
    fine = Mesh(mesh.devices.reshape(sizes), names)
    return jax.shard_map(
        body,
        mesh=fine,
        in_specs=(
            P(SAMPLE, TENSOR),
            P(SAMPLE, TENSOR),
            P(),
            P(None, TENSOR),
            P(None, TENSOR),
            P(None, TENSOR),
            P(TENSOR, None),
            P(SAMPLE),
            P(),
        ),
        out_specs=P(SAMPLE, TENSOR),
        check_vma=False,
    )
```

```python
import functools
import math

import jax
import jax.numpy as jnp
from jax import lax
from jax.experimental import pallas as pl
from jax.experimental.pallas import tpu as pltpu
from jax.sharding import Mesh
from jax.sharding import PartitionSpec as P

PARTS = (("xh", 2), ("y", 4), ("core", 2), ("k", 4), ("zl", 2), ("xl", 2))
SAMPLE = ("xh", "y", "core")
TENSOR = ("k", "zl", "xl")
ZRING = ("k", "zl")
KEY_GROUP = ("xh", "core", "zl", "xl")

D = 8192
BLOCK = 512
HEAD_DIM = 128
HALF = 64
RESP = 64
PROMPT_ROWS = 256
ROWS = 160
SHARED_ROWS = 144
SENT_ROWS = ROWS + 16
PACKED = 64 + RESP
EPSILON = 1e-05
ROPE_BASE = 500000.0
NEG_BIG = -1e30
CORE_AT, XL_AT, T_AT, Y_AT, PLACE_AT, LENGTH_AT = 0, 1, 2, 3, 4, 5
F32 = jnp.float32
BF16 = jnp.bfloat16
SMALL = 12 * 1024 * 1024


def iota(shape, dim):
    return lax.broadcasted_iota(jnp.int32, shape, dim)


def dot_t(a, b):
    return lax.dot_general(a, b, (((1,), (1,)), ((), ())), preferred_element_type=F32)


def dot(a, b):
    return lax.dot_general(a, b, (((1,), (0,)), ((), ())), preferred_element_type=F32)


LONG = pl.CostEstimate(flops=30_000_000_000, bytes_accessed=1_000_000, transcendentals=0)


def params(limit=None):
    return pltpu.CompilerParams(vmem_limit_bytes=limit)


def pack_kernel(core_ref, key_ref, value_ref, hidden_ref, out_ref):
    for i in range(out_ref.shape[0]):
        for x in range(2):
            at = (2 * i + x) * BLOCK
            out_ref[i, 32 * x : 32 * x + 16] = key_ref[:, at : at + BLOCK]
            out_ref[i, 32 * x + 16 : 32 * x + 32] = value_ref[:, at : at + BLOCK]
        out_ref[i, 64:] = hidden_ref[...]


def pack(core, key_rows, value_rows, hidden):
    steps = 2
    each = 8 // steps
    rows = pl.BlockSpec((16, 2 * each * BLOCK), lambda i, core: (core[0], i))
    return pl.pallas_call(
        pack_kernel,
        grid_spec=pltpu.PrefetchScalarGridSpec(
            num_scalar_prefetch=1,
            grid=(steps,),
            in_specs=[rows, rows, pl.BlockSpec((RESP, BLOCK), lambda i, core: (0, 0))],
            out_specs=pl.BlockSpec((each, PACKED, BLOCK), lambda i, core: (i, 0, 0)),
        ),
        out_shape=jax.ShapeDtypeStruct((8, PACKED, BLOCK), BF16),
        compiler_params=params(),
        name="pack",
    )(core, key_rows, value_rows, hidden)


def scale_kernel(info_ref, prompt_ref, resp_ref, gain_ref, out_ref, high, low):
    gain = gain_ref[info_ref[T_AT]]

    def put(at, count, values):
        values = values.astype(F32)
        out_ref[at : at + count] = (values * gain).astype(BF16)
        square = values * values
        top = square.astype(BF16)
        high[at : at + count] = top
        low[at : at + count] = (square - top.astype(F32)).astype(BF16)

    for half in range(2):
        put(ROWS * half, 128, prompt_ref[128 * half : 128 * half + 128])
        put(ROWS * half + 128, 32, resp_ref[32 * half : 32 * half + 32])
    high[320:448] = jnp.zeros((128, BLOCK), BF16)
    low[320:448] = jnp.zeros((128, BLOCK), BF16)
    ones = jnp.ones((16, BLOCK), BF16)
    row = iota((16, 128), 0)
    rows = jnp.zeros((16, 128), F32)
    for n, at in enumerate((0, 128, ROWS, ROWS + 128)):
        total = dot_t(ones, high[at : at + 128]) + dot_t(ones, low[at : at + 128])
        top = total.astype(BF16).astype(F32)
        rows = jnp.where(row == 2 * n, top, jnp.where(row == 2 * n + 1, total - top, rows))
    out_ref[320:, :128] = rows.astype(BF16)
    out_ref[320:, 128:] = jnp.zeros((16, BLOCK - 128), BF16)


def scale_rows(info, prompt, resp, gain):
    vmem = pl.BlockSpec(memory_space=pltpu.VMEM)
    return pl.pallas_call(
        scale_kernel,
        in_specs=[pl.BlockSpec(memory_space=pltpu.SMEM), vmem, vmem, vmem],
        out_shape=jax.ShapeDtypeStruct((2 * ROWS + 16, BLOCK), BF16),
        scratch_shapes=[pltpu.VMEM((448, BLOCK), BF16), pltpu.VMEM((448, BLOCK), BF16)],
        compiler_params=params(SMALL),
        name="scale_rows",
    )(info, prompt, resp, gain)


def split_kernel(got_ref, *refs):
    refs[-1][...] = got_ref[:, 64:]


def split(got, after):
    return pl.pallas_call(
        split_kernel,
        in_specs=[pl.BlockSpec(memory_space=pltpu.VMEM)] * (1 + len(after)),
        out_shape=jax.ShapeDtypeStruct((8, RESP, BLOCK), BF16),
        compiler_params=params(SMALL),
        name="split",
    )(got, *after)


def partial_kernel(info_ref, got_ref, *refs):
    out_ref = refs[4]
    xl, core = info_ref[XL_AT], info_ref[CORE_AT]
    weights = [got_ref[:, pl.ds(pl.multiple_of(32 * x, 32), 32)].reshape(256, BLOCK) for x in (xl, 1 - xl)]
    row, col = iota((256, 512), 0), iota((256, 512), 1)
    target = (row & 3) * 128 + (row >> 5) * 8 + ((row >> 2) & 7)
    total = jnp.zeros((2 * ROWS, 512), F32)
    sums = []
    for n, at in enumerate((core, 1 - core)):
        here, there = refs[2 * n], refs[2 * n + 1]
        raw = dot_t(here[: 2 * ROWS], weights[0]) + dot_t(there[: 2 * ROWS], weights[1])
        pick = jnp.where(col == target + 64 * at, 1.0, 0.0).astype(BF16)
        total += dot(raw.astype(BF16), pick)
        sums.append((here[2 * ROWS :, :128], there[2 * ROWS :, :128]))
    total = total.astype(BF16)
    for half in range(2):
        lines = [[piece[4 * half : 4 * half + 4] for piece in pair] for pair in sums]
        lines = [jnp.concatenate(lines[0] + lines[1], axis=0), jnp.concatenate(lines[1] + lines[0], axis=0)]
        for head in range(4):
            to = 2 * head + half
            out_ref[to, :ROWS] = total[ROWS * half : ROWS * half + ROWS, head * 128 : head * 128 + 128]
            out_ref[to, ROWS:] = jnp.where(core == 0, lines[0], lines[1])


def partial_products(info, got, blocks):
    vmem = pl.BlockSpec(memory_space=pltpu.VMEM)
    return pl.pallas_call(
        partial_kernel,
        in_specs=[pl.BlockSpec(memory_space=pltpu.SMEM)] + [vmem] * 5,
        out_shape=jax.ShapeDtypeStruct((8, SENT_ROWS, 128), BF16),
        compiler_params=params(SMALL),
        name="partial_products",
    )(info, got, *blocks)


def turn(values, cosine, sine):
    return values * cosine + pltpu.roll(values, HALF, 1) * sine


def finish_kernel(parts_ref, trig_ref, *refs):
    out_ref = refs[-1]
    total = jnp.sum(parts_ref[...].astype(F32), axis=0)
    sums = total[ROWS:]
    factors = []
    for core in range(2):
        column = []
        for n, count in enumerate((128, ROWS - 128)):
            at = 8 * core + 2 * n
            line = sums[at : at + 1] + sums[at + 1 : at + 2] + sums[at + 4 : at + 5] + sums[at + 5 : at + 6]
            diagonal = iota((count, 128), 0) == iota((count, 128), 1)
            spread = jnp.where(diagonal, jnp.broadcast_to(line, (count, 128)), 0.0)
            column.append(jnp.sum(spread, axis=1, keepdims=True))
        factors.append(lax.rsqrt(jnp.concatenate(column, axis=0) * (1.0 / D) + EPSILON))
    factor = jnp.where(iota((ROWS, 128), 1) < 64, factors[0], factors[1])
    raw = (total[:ROWS] * factor).astype(BF16)
    row, col = iota((128, 128), 0), iota((128, 128), 1)
    target = (row & 64) + ((row >> 2) & 1) * 32 + ((row >> 3) & 7) * 4 + (row & 3)
    ordered = dot(raw, jnp.where(col == target, 1.0, 0.0).astype(BF16))
    beside = dot(raw, jnp.where(col == (target ^ 16), 1.0, 0.0).astype(BF16))
    result = ordered * trig_ref[0, :ROWS] + beside * trig_ref[1, :ROWS]
    prompt = result[:128].astype(BF16)
    first, second = result[128:144], result[144:160]
    left = iota((16, 128), 1) < 64
    resp = (
        jnp.where(left, first, pltpu.roll(second, 64, 1)).astype(BF16),
        jnp.where(left, pltpu.roll(first, 64, 1), second).astype(BF16),
    )
    for i in range(out_ref.shape[0]):
        out_ref[i, :128] = prompt
        out_ref[i, 128:] = resp[(i >> 2) & 1]


def finish_keys(parts, trig, *after):
    return pl.pallas_call(
        finish_kernel,
        in_specs=[pl.BlockSpec(memory_space=pltpu.VMEM)] * (2 + len(after)),
        out_shape=jax.ShapeDtypeStruct((16, SHARED_ROWS, 128), BF16),
        compiler_params=params(SMALL),
        cost_estimate=LONG,
        name="finish_keys",
    )(parts, trig, *after)


def by_device(natural):
    return ((natural >> 3) & 1) * 64 + ((natural >> 2) & 1) * 32 + (natural >> 4) * 4 + (natural & 3)


def query_kernel(info_ref, gain_ref, trig_ref, weight_ref, own_ref, other_ref, out_ref):
    xl = info_ref[XL_AT]
    total = jnp.zeros((RESP, 256), F32)
    squares = jnp.zeros((RESP, 1), F32)
    for z in range(8):
        for j, ref in enumerate((own_ref, other_ref)):
            x = j ^ xl
            hidden = ref[z].astype(F32)
            scaled = (hidden * gain_ref[2 * z + x]).astype(BF16)
            total += dot(scaled, weight_ref[pl.ds(pl.multiple_of((2 * z + x) * BLOCK, BLOCK), BLOCK)])
            squares += jnp.sum(hidden * hidden, axis=1, keepdims=True)
    factor = lax.rsqrt(squares * (1.0 / D) + EPSILON)
    row, col = iota((128, 128), 0), iota((128, 128), 1)
    order = jnp.where(col == by_device(row), 1.0, 0.0).astype(BF16)
    for h in range(2):
        part = slice(h * HEAD_DIM, (h + 1) * HEAD_DIM)
        query = turn(total[:, part] * factor, trig_ref[0, ROWS:], trig_ref[1, ROWS:])
        out_ref[:, part] = dot(query.astype(BF16), order).astype(BF16)


def queries_of(info, gain, weight, trig, own, other):
    vmem = pl.BlockSpec(memory_space=pltpu.VMEM)
    return pl.pallas_call(
        query_kernel,
        in_specs=[pl.BlockSpec(memory_space=pltpu.SMEM)] + [vmem] * 5,
        out_shape=jax.ShapeDtypeStruct((RESP, 256), BF16),
        compiler_params=params(SMALL),
        cost_estimate=LONG,
        name="queries",
    )(info, gain, trig, weight, own, other)


def attend_kernel(info_ref, rows_ref, *refs):
    queries, outs = refs[:4], refs[4:]
    own_y = info_ref[Y_AT]

    def joined(xh, zl, at, count):
        group = iota((count, 128), 1) >> 5
        pieces = [
            rows_ref[xh * 8 + core * 4 + zl * 2 + x, at : at + count].astype(F32) for x in range(2) for core in range(2)
        ]
        result = []
        for g in range(4):
            rows = pltpu.roll(pieces[0], (-32 * g) % 128, 1) if g else pieces[0]
            for p in range(1, 4):
                shift = (32 * (p - g)) % 128
                rows = jnp.where(group == p, pltpu.roll(pieces[p], shift, 1) if shift else pieces[p], rows)
            result.append(rows.astype(BF16))
        return result

    prompt = [[joined(xh, zl, 0, 128) for zl in range(2)] for xh in range(2)]

    def prompt_rows(kv):
        return jnp.concatenate(
            [prompt[xh][zl][2 * core + kv] for xh in range(2) for core in range(2) for zl in range(2)], axis=0
        )

    prompt_keys, prompt_values = prompt_rows(0), prompt_rows(1)
    own_xh = info_ref[PLACE_AT] // 2
    own = [joined(own_xh, zl, 128, 16) for zl in range(2)]

    def own_rows(kv):
        return jnp.concatenate([o[2 * n + kv] for o in own for n in range(2)], axis=0)

    own_keys, own_values = own_rows(0), own_rows(1)
    scale = HEAD_DIM ** (-0.5)
    power = scale * math.log2(math.e)

    column = iota((1, 1024), 1)
    sample = (column >> 9) * 8 + own_y * 2 + ((column >> 8) & 1)
    live = sample * PROMPT_ROWS + (column & 255) < info_ref[LENGTH_AT]
    causal = iota((2 * RESP, RESP), 1) <= (iota((2 * RESP, RESP), 0) & (RESP - 1))
    lane = iota((RESP, 128), 1)

    query = jnp.concatenate([q[:, h * HEAD_DIM : (h + 1) * HEAD_DIM] for q in queries for h in range(2)], axis=0)
    mine = 2 * RESP
    far = jnp.where(live, dot_t(query, prompt_keys), NEG_BIG)
    near = jnp.where(causal, dot_t(query[:mine], own_keys), NEG_BIG)
    top = jnp.max(far, axis=1, keepdims=True)
    top_mine = jnp.maximum(top[:mine], jnp.max(near, axis=1, keepdims=True))
    top = jnp.maximum(jnp.concatenate([top_mine, top[mine:]], axis=0), 0.5 * NEG_BIG)
    far = jnp.exp2((far - top) * power)
    near = jnp.exp2((near - top[:mine]) * power)
    total = jnp.sum(far, axis=1, keepdims=True)
    total = jnp.concatenate([total[:mine] + jnp.sum(near, axis=1, keepdims=True), total[mine:]], axis=0)
    summed = dot(far.astype(BF16), prompt_values)
    summed = jnp.concatenate([summed[:mine] + dot(near.astype(BF16), own_values), summed[mine:]], axis=0)
    some = total > 0.0
    safe = jnp.where(some, total, 1.0)
    result = (summed / safe).astype(BF16)
    level = jnp.where(some, top * scale + jnp.log(safe), NEG_BIG)
    first = level.astype(BF16).astype(F32)
    rest = level - first
    second = rest.astype(BF16).astype(F32)
    third = rest - second
    for i in range(4):
        extra = jnp.zeros((RESP, 128), F32)
        for h in range(2):
            at = slice((2 * i + h) * RESP, (2 * i + h + 1) * RESP)
            outs[i][:, h * HEAD_DIM : (h + 1) * HEAD_DIM] = result[at]
            for n, piece in enumerate((first, second, third)):
                extra = jnp.where(lane == 3 * h + n, piece[at], extra)
        outs[i][:, 256:] = extra.astype(BF16)


def attend(info, rows, queries):
    vmem = pl.BlockSpec(memory_space=pltpu.VMEM)
    return pl.pallas_call(
        attend_kernel,
        in_specs=[pl.BlockSpec(memory_space=pltpu.SMEM)] + [vmem] * 5,
        out_shape=(jax.ShapeDtypeStruct((RESP, 384), BF16),) * 4,
        compiler_params=params(SMALL),
        name="attend",
    )(info, rows, *queries)


def merge_kernel(*refs):
    parts, out_ref = refs[:4], refs[4]
    lane = iota((RESP, 128), 1)
    row, col = iota((128, 128), 0), iota((128, 128), 1)
    order = jnp.where(row == by_device(col), 1.0, 0.0).astype(BF16)
    extras = [part[:, 256:].astype(F32) for part in parts]
    for h in range(2):
        head = slice(h * HEAD_DIM, (h + 1) * HEAD_DIM)
        mine = jnp.logical_and(lane >= 3 * h, lane < 3 * h + 3)
        levels = [jnp.sum(jnp.where(mine, e, 0.0), axis=1, keepdims=True) for e in extras]
        top = functools.reduce(jnp.maximum, levels)
        shares = [jnp.exp(level - top) for level in levels]
        total = functools.reduce(jnp.add, shares)
        pieces = [share * part[:, head].astype(F32) for share, part in zip(shares, parts)]
        mean = (functools.reduce(jnp.add, pieces) / total).astype(BF16)
        out_ref[:, head] = dot(mean, order).astype(BF16)


def merge(parts):
    vmem = pl.BlockSpec(memory_space=pltpu.VMEM)
    return pl.pallas_call(
        merge_kernel,
        in_specs=[vmem] * 4,
        out_shape=jax.ShapeDtypeStruct((RESP, 256), BF16),
        compiler_params=params(SMALL),
        name="merge",
    )(*parts)


def z_of(i, info):
    return (4 * info[CORE_AT]) ^ i


def project_own_kernel(info_ref, own_ref, weight_ref, out_ref):
    for i in range(8):
        at = (2 * z_of(i, info_ref) + info_ref[XL_AT]) * BLOCK
        out_ref[i] = dot(own_ref[...], weight_ref[:, pl.ds(pl.multiple_of(at, BLOCK), BLOCK)])


def project_own(info, own, weight):
    vmem = pl.BlockSpec(memory_space=pltpu.VMEM)
    return pl.pallas_call(
        project_own_kernel,
        in_specs=[pl.BlockSpec(memory_space=pltpu.SMEM)] + [vmem] * 2,
        out_shape=jax.ShapeDtypeStruct((8, RESP, BLOCK), F32),
        compiler_params=params(SMALL),
        cost_estimate=LONG,
        name="project_own",
    )(info, own, weight)


def project_kernel(info_ref, started_ref, other_ref, *refs):
    cross, out_ref = refs[:4], refs[4]
    for i in range(8):
        result = started_ref[i] + dot(other_ref[...], cross[i // 2][:, pl.ds((i % 2) * BLOCK, BLOCK)])
        out_ref[z_of(i, info_ref)] = result.astype(BF16)


def project(info, started, other, cross):
    vmem = pl.BlockSpec(memory_space=pltpu.VMEM)
    return pl.pallas_call(
        project_kernel,
        in_specs=[pl.BlockSpec(memory_space=pltpu.SMEM)] + [vmem] * 6,
        out_shape=jax.ShapeDtypeStruct((8, RESP, BLOCK), BF16),
        compiler_params=params(SMALL),
        name="project",
    )(info, started, other, *cross)


def pick_kernel(info_ref, weight_ref, after_ref, *out_refs):
    for i in range(4):
        at = (2 * z_of(i, info_ref) + 1 - info_ref[XL_AT]) * BLOCK
        columns = weight_ref[:, pl.ds(pl.multiple_of(at, BLOCK), BLOCK)]
        out_refs[i // 2][:, (i % 2) * BLOCK : (i % 2) * BLOCK + BLOCK] = columns


def pick_columns(info, weight, after):
    vmem = pl.BlockSpec(memory_space=pltpu.VMEM)
    return pl.pallas_call(
        pick_kernel,
        in_specs=[pl.BlockSpec(memory_space=pltpu.SMEM)] + [vmem] * 2,
        out_shape=(jax.ShapeDtypeStruct((256, 2 * BLOCK), BF16),) * 2,
        compiler_params=params(SMALL),
        name="pick_columns",
    )(info, weight, after)


def swap(values, axis):
    return lax.all_to_all(values, axis, 0, 0, tiled=False)


def body(
    response_hidden,
    prompt_hidden,
    norm_gain,
    query_weight,
    key_weight,
    value_weight,
    output_weight,
    response_lengths,
    prompt_length,
):
    length = prompt_length[0]
    core, y = lax.axis_index("core"), lax.axis_index("y")
    sample, half, xl = lax.axis_index(SAMPLE), lax.axis_index("zl"), lax.axis_index("xl")
    gain = norm_gain.astype(F32).reshape(16, 1, BLOCK)

    row = jnp.arange(ROWS + RESP, dtype=jnp.int32)[:, None]
    lane = jnp.arange(HEAD_DIM, dtype=jnp.int32)[None, :]
    sample_of = sample - core + (lane >> 6)
    positions = jnp.where(
        row < 128,
        sample_of * PROMPT_ROWS + half * 128 + row,
        jnp.where(row < ROWS, length + half * 32 + row - 128, length + row - ROWS),
    )
    entry = (2 * ((lane >> 2) & 7) + xl) * 8 + 4 * core + (lane & 3)
    entry = jnp.where(row < ROWS, entry, lane)
    still = (row < ROWS) & ((lane & 32) > 0)
    inverse = ROPE_BASE ** (-((entry % HALF).astype(F32) * 2.0 / HEAD_DIM))
    angles = jnp.where(still, 0.0, positions.astype(F32) * inverse)
    trig = jnp.stack([jnp.cos(angles), jnp.sin(angles) * jnp.where(entry < HALF, -1.0, 1.0)])

    info = jnp.stack(
        [core, xl, lax.axis_index(TENSOR), y, lax.axis_index(("xh", "core")), length]
    ).astype(jnp.int32)
    flip = [(0, 1), (1, 0)]

    packed = pack(core.reshape(1), key_weight.T, value_weight.T, response_hidden)
    got = swap(packed, ZRING)
    scaled = scale_rows(info, prompt_hidden, response_hidden, gain)
    beside = lax.ppermute(scaled, "xl", flip)
    crossed = lax.ppermute(scaled, "core", flip), lax.ppermute(beside, "core", flip)
    sent = pick_columns(info, output_weight, scaled)
    early, late = (lax.ppermute(piece, "xl", flip) for piece in sent)
    own_hidden = split(got, (*crossed, early, sent[1], trig))
    other_hidden = lax.ppermute(own_hidden, "xl", flip)
    products = partial_products(info, got, (scaled, beside, *crossed))
    products = swap(products, ZRING)
    queries = queries_of(info, gain, query_weight, trig, own_hidden, other_hidden)
    cross = (early, late, lax.ppermute(early, "core", flip), lax.ppermute(late, "core", flip))
    rows = finish_keys(products, trig, queries)
    rows = swap(rows, KEY_GROUP)

    def along(values, step):
        return lax.ppermute(values, "y", [(i, (i + step) % 4) for i in range(4)])

    pooled = [queries] + [along(queries, step) for step in (1, 2, 3)]
    parts = attend(info, rows, pooled)
    attention = merge([parts[0]] + [along(parts[step], -step) for step in (1, 2, 3)])
    partner = lax.ppermute(attention, "xl", flip)
    partial = project(info, project_own(info, attention, output_weight), partner, cross)
    summed = jnp.sum(swap(partial, ZRING).astype(F32), axis=0)
    live = jnp.arange(RESP, dtype=jnp.int32) < response_lengths[0]
    return jnp.where(live[:, None], summed, 0.0).astype(BF16)


def solution(mesh):
    names = tuple(name for name, _ in PARTS)
    sizes = tuple(size for _, size in PARTS)
    fine = Mesh(mesh.devices.reshape(sizes), names)
    return jax.shard_map(
        body,
        mesh=fine,
        in_specs=(
            P(SAMPLE, TENSOR),
            P(SAMPLE, TENSOR),
            P(),
            P(None, TENSOR),
            P(None, TENSOR),
            P(None, TENSOR),
            P(TENSOR, None),
            P(SAMPLE),
            P(),
        ),
        out_specs=P(SAMPLE, TENSOR),
        check_vma=False,
    )
```

```python
import functools
import math

import jax
import jax.numpy as jnp
from jax import lax
from jax.experimental import pallas as pl
from jax.experimental.pallas import tpu as pltpu
from jax.sharding import Mesh
from jax.sharding import PartitionSpec as P

PARTS = (("xh", 2), ("y", 4), ("core", 2), ("k", 4), ("zl", 2), ("xl", 2))
SAMPLE = ("xh", "y", "core")
TENSOR = ("k", "zl", "xl")
ZRING = ("k", "zl")
KEY_GROUP = ("xh", "core", "zl", "xl")

D = 8192
BLOCK = 512
HEAD_DIM = 128
HALF = 64
RESP = 64
PROMPT_ROWS = 256
ROWS = 160
SHARED_ROWS = 144
SENT_ROWS = ROWS + 16
PACKED = 64 + RESP
EPSILON = 1e-05
ROPE_BASE = 500000.0
NEG_BIG = -1e30
CORE_AT, XL_AT, T_AT, Y_AT, PLACE_AT, LENGTH_AT = 0, 1, 2, 3, 4, 5
F32 = jnp.float32
BF16 = jnp.bfloat16
SMALL = 12 * 1024 * 1024


def iota(shape, dim):
    return lax.broadcasted_iota(jnp.int32, shape, dim)


def dot_t(a, b):
    return lax.dot_general(a, b, (((1,), (1,)), ((), ())), preferred_element_type=F32)


def dot(a, b):
    return lax.dot_general(a, b, (((1,), (0,)), ((), ())), preferred_element_type=F32)


LONG = pl.CostEstimate(flops=30_000_000_000, bytes_accessed=1_000_000, transcendentals=0)


def params(limit=None):
    return pltpu.CompilerParams(vmem_limit_bytes=limit)


def pack_kernel(core_ref, key_ref, value_ref, hidden_ref, out_ref):
    for i in range(out_ref.shape[0]):
        for x in range(2):
            at = (2 * i + x) * BLOCK
            out_ref[i, 32 * x : 32 * x + 16] = key_ref[:, at : at + BLOCK]
            out_ref[i, 32 * x + 16 : 32 * x + 32] = value_ref[:, at : at + BLOCK]
        out_ref[i, 64:] = hidden_ref[...]


def pack(core, key_rows, value_rows, hidden):
    steps = 2
    each = 8 // steps
    rows = pl.BlockSpec((16, 2 * each * BLOCK), lambda i, core: (core[0], i))
    return pl.pallas_call(
        pack_kernel,
        grid_spec=pltpu.PrefetchScalarGridSpec(
            num_scalar_prefetch=1,
            grid=(steps,),
            in_specs=[rows, rows, pl.BlockSpec((RESP, BLOCK), lambda i, core: (0, 0))],
            out_specs=pl.BlockSpec((each, PACKED, BLOCK), lambda i, core: (i, 0, 0)),
        ),
        out_shape=jax.ShapeDtypeStruct((8, PACKED, BLOCK), BF16),
        compiler_params=params(),
        name="pack",
    )(core, key_rows, value_rows, hidden)


def scale_kernel(info_ref, prompt_ref, resp_ref, gain_ref, out_ref, high, low):
    gain = gain_ref[info_ref[T_AT]]

    def put(at, count, values):
        values = values.astype(F32)
        out_ref[at : at + count] = (values * gain).astype(BF16)
        square = values * values
        top = square.astype(BF16)
        high[at : at + count] = top
        low[at : at + count] = (square - top.astype(F32)).astype(BF16)

    for half in range(2):
        put(ROWS * half, 128, prompt_ref[128 * half : 128 * half + 128])
        put(ROWS * half + 128, 32, resp_ref[32 * half : 32 * half + 32])
    high[320:448] = jnp.zeros((128, BLOCK), BF16)
    low[320:448] = jnp.zeros((128, BLOCK), BF16)
    ones = jnp.ones((16, BLOCK), BF16)
    row = iota((16, 128), 0)
    rows = jnp.zeros((16, 128), F32)
    for n, at in enumerate((0, 128, ROWS, ROWS + 128)):
        total = dot_t(ones, high[at : at + 128]) + dot_t(ones, low[at : at + 128])
        top = total.astype(BF16).astype(F32)
        rows = jnp.where(row == 2 * n, top, jnp.where(row == 2 * n + 1, total - top, rows))
    out_ref[320:, :128] = rows.astype(BF16)
    out_ref[320:, 128:] = jnp.zeros((16, BLOCK - 128), BF16)


def scale_rows(info, prompt, resp, gain):
    vmem = pl.BlockSpec(memory_space=pltpu.VMEM)
    return pl.pallas_call(
        scale_kernel,
        in_specs=[pl.BlockSpec(memory_space=pltpu.SMEM), vmem, vmem, vmem],
        out_shape=jax.ShapeDtypeStruct((2 * ROWS + 16, BLOCK), BF16),
        scratch_shapes=[pltpu.VMEM((448, BLOCK), BF16), pltpu.VMEM((448, BLOCK), BF16)],
        compiler_params=params(SMALL),
        name="scale_rows",
    )(info, prompt, resp, gain)


def split_kernel(got_ref, *refs):
    refs[-1][...] = got_ref[:, 64:]


def split(got, after):
    return pl.pallas_call(
        split_kernel,
        in_specs=[pl.BlockSpec(memory_space=pltpu.VMEM)] * (1 + len(after)),
        out_shape=jax.ShapeDtypeStruct((8, RESP, BLOCK), BF16),
        compiler_params=params(SMALL),
        name="split",
    )(got, *after)


def partial_kernel(info_ref, got_ref, *refs):
    out_ref = refs[4]
    xl, core = info_ref[XL_AT], info_ref[CORE_AT]
    weights = [got_ref[:, pl.ds(pl.multiple_of(32 * x, 32), 32)].reshape(256, BLOCK) for x in (xl, 1 - xl)]
    row, col = iota((256, 512), 0), iota((256, 512), 1)
    target = (row & 3) * 128 + (row >> 5) * 8 + ((row >> 2) & 7)
    total = jnp.zeros((2 * ROWS, 512), F32)
    sums = []
    for n, at in enumerate((core, 1 - core)):
        here, there = refs[2 * n], refs[2 * n + 1]
        raw = dot_t(here[: 2 * ROWS], weights[0]) + dot_t(there[: 2 * ROWS], weights[1])
        pick = jnp.where(col == target + 64 * at, 1.0, 0.0).astype(BF16)
        total += dot(raw.astype(BF16), pick)
        sums.append((here[2 * ROWS :, :128], there[2 * ROWS :, :128]))
    total = total.astype(BF16)
    for half in range(2):
        lines = [[piece[4 * half : 4 * half + 4] for piece in pair] for pair in sums]
        lines = [jnp.concatenate(lines[0] + lines[1], axis=0), jnp.concatenate(lines[1] + lines[0], axis=0)]
        for head in range(4):
            to = 2 * head + half
            out_ref[to, :ROWS] = total[ROWS * half : ROWS * half + ROWS, head * 128 : head * 128 + 128]
            out_ref[to, ROWS:] = jnp.where(core == 0, lines[0], lines[1])


def partial_products(info, got, blocks):
    vmem = pl.BlockSpec(memory_space=pltpu.VMEM)
    return pl.pallas_call(
        partial_kernel,
        in_specs=[pl.BlockSpec(memory_space=pltpu.SMEM)] + [vmem] * 5,
        out_shape=jax.ShapeDtypeStruct((8, SENT_ROWS, 128), BF16),
        compiler_params=params(SMALL),
        name="partial_products",
    )(info, got, *blocks)


def turn(values, cosine, sine):
    return values * cosine + pltpu.roll(values, HALF, 1) * sine


def finish_kernel(parts_ref, trig_ref, *refs):
    out_ref, shared, sems = refs[-3:]
    total = jnp.sum(parts_ref[...].astype(F32), axis=0)
    sums = total[ROWS:]
    factors = []
    for core in range(2):
        column = []
        for n, count in enumerate((128, ROWS - 128)):
            at = 8 * core + 2 * n
            line = sums[at : at + 1] + sums[at + 1 : at + 2] + sums[at + 4 : at + 5] + sums[at + 5 : at + 6]
            diagonal = iota((count, 128), 0) == iota((count, 128), 1)
            spread = jnp.where(diagonal, jnp.broadcast_to(line, (count, 128)), 0.0)
            column.append(jnp.sum(spread, axis=1, keepdims=True))
        factors.append(lax.rsqrt(jnp.concatenate(column, axis=0) * (1.0 / D) + EPSILON))
    factor = jnp.where(iota((ROWS, 128), 1) < 64, factors[0], factors[1])
    raw = (total[:ROWS] * factor).astype(BF16)
    row, col = iota((128, 128), 0), iota((128, 128), 1)
    target = (row & 64) + ((row >> 2) & 1) * 32 + ((row >> 3) & 7) * 4 + (row & 3)
    ordered = dot(raw, jnp.where(col == target, 1.0, 0.0).astype(BF16))
    beside = dot(raw, jnp.where(col == (target ^ 16), 1.0, 0.0).astype(BF16))
    result = ordered * trig_ref[0, :ROWS] + beside * trig_ref[1, :ROWS]
    prompt = result[:128].astype(BF16)
    first, second = result[128:144], result[144:160]
    left = iota((16, 128), 1) < 64
    resp = (
        jnp.where(left, first, pltpu.roll(second, 64, 1)).astype(BF16),
        jnp.where(left, pltpu.roll(first, 64, 1), second).astype(BF16),
    )
    for core in range(2):
        shared[core, :128] = prompt
        shared[core, 128:] = resp[core]
    copies = [pltpu.make_async_copy(shared.at[(i >> 2) & 1], out_ref.at[i], sems.at[i]) for i in range(16)]
    for copy in copies:
        copy.start()
    for copy in copies:
        copy.wait()


def finish_keys(parts, trig, *after):
    return pl.pallas_call(
        finish_kernel,
        in_specs=[pl.BlockSpec(memory_space=pltpu.VMEM)] * (2 + len(after)),
        out_specs=pl.BlockSpec(memory_space=pl.ANY),
        out_shape=jax.ShapeDtypeStruct((16, SHARED_ROWS, 128), BF16),
        scratch_shapes=[pltpu.VMEM((2, SHARED_ROWS, 128), BF16), pltpu.SemaphoreType.DMA((16,))],
        compiler_params=params(SMALL),
        cost_estimate=LONG,
        name="finish_keys",
    )(parts, trig, *after)


def by_device(natural):
    return ((natural >> 3) & 1) * 64 + ((natural >> 2) & 1) * 32 + (natural >> 4) * 4 + (natural & 3)


def query_kernel(info_ref, gain_ref, trig_ref, weight_ref, own_ref, other_ref, out_ref):
    xl = info_ref[XL_AT]
    total = jnp.zeros((RESP, 256), F32)
    squares = jnp.zeros((RESP, 1), F32)
    for z in range(8):
        for j, ref in enumerate((own_ref, other_ref)):
            x = j ^ xl
            hidden = ref[z].astype(F32)
            scaled = (hidden * gain_ref[2 * z + x]).astype(BF16)
            total += dot(scaled, weight_ref[pl.ds(pl.multiple_of((2 * z + x) * BLOCK, BLOCK), BLOCK)])
            squares += jnp.sum(hidden * hidden, axis=1, keepdims=True)
    factor = lax.rsqrt(squares * (1.0 / D) + EPSILON)
    row, col = iota((128, 128), 0), iota((128, 128), 1)
    order = jnp.where(col == by_device(row), 1.0, 0.0).astype(BF16)
    for h in range(2):
        part = slice(h * HEAD_DIM, (h + 1) * HEAD_DIM)
        query = turn(total[:, part] * factor, trig_ref[0, ROWS:], trig_ref[1, ROWS:])
        out_ref[:, part] = dot(query.astype(BF16), order).astype(BF16)


def queries_of(info, gain, weight, trig, own, other):
    vmem = pl.BlockSpec(memory_space=pltpu.VMEM)
    return pl.pallas_call(
        query_kernel,
        in_specs=[pl.BlockSpec(memory_space=pltpu.SMEM)] + [vmem] * 5,
        out_shape=jax.ShapeDtypeStruct((RESP, 256), BF16),
        compiler_params=params(SMALL),
        cost_estimate=LONG,
        name="queries",
    )(info, gain, trig, weight, own, other)


def attend_kernel(info_ref, rows_ref, *refs):
    queries, outs = refs[:4], refs[4:]
    own_y = info_ref[Y_AT]

    def joined(xh, zl, at, count):
        group = iota((count, 128), 1) >> 5
        pieces = [
            rows_ref[xh * 8 + core * 4 + zl * 2 + x, at : at + count].astype(F32) for x in range(2) for core in range(2)
        ]
        result = []
        for g in range(4):
            rows = pltpu.roll(pieces[0], (-32 * g) % 128, 1) if g else pieces[0]
            for p in range(1, 4):
                shift = (32 * (p - g)) % 128
                rows = jnp.where(group == p, pltpu.roll(pieces[p], shift, 1) if shift else pieces[p], rows)
            result.append(rows.astype(BF16))
        return result

    prompt = [[joined(xh, zl, 0, 128) for zl in range(2)] for xh in range(2)]

    def prompt_rows(kv):
        return jnp.concatenate(
            [prompt[xh][zl][2 * core + kv] for xh in range(2) for core in range(2) for zl in range(2)], axis=0
        )

    prompt_keys, prompt_values = prompt_rows(0), prompt_rows(1)
    own_xh = info_ref[PLACE_AT] // 2
    own = [joined(own_xh, zl, 128, 16) for zl in range(2)]

    def own_rows(kv):
        return jnp.concatenate([o[2 * n + kv] for o in own for n in range(2)], axis=0)

    own_keys, own_values = own_rows(0), own_rows(1)
    scale = HEAD_DIM ** (-0.5)
    power = scale * math.log2(math.e)

    column = iota((1, 1024), 1)
    sample = (column >> 9) * 8 + own_y * 2 + ((column >> 8) & 1)
    live = sample * PROMPT_ROWS + (column & 255) < info_ref[LENGTH_AT]
    causal = iota((2 * RESP, RESP), 1) <= (iota((2 * RESP, RESP), 0) & (RESP - 1))
    lane = iota((RESP, 128), 1)

    query = jnp.concatenate([q[:, h * HEAD_DIM : (h + 1) * HEAD_DIM] for q in queries for h in range(2)], axis=0)
    mine = 2 * RESP
    far = jnp.where(live, dot_t(query, prompt_keys), NEG_BIG)
    near = jnp.where(causal, dot_t(query[:mine], own_keys), NEG_BIG)
    top = jnp.max(far, axis=1, keepdims=True)
    top_mine = jnp.maximum(top[:mine], jnp.max(near, axis=1, keepdims=True))
    top = jnp.maximum(jnp.concatenate([top_mine, top[mine:]], axis=0), 0.5 * NEG_BIG)
    far = jnp.exp2((far - top) * power)
    near = jnp.exp2((near - top[:mine]) * power)
    total = jnp.sum(far, axis=1, keepdims=True)
    total = jnp.concatenate([total[:mine] + jnp.sum(near, axis=1, keepdims=True), total[mine:]], axis=0)
    summed = dot(far.astype(BF16), prompt_values)
    summed = jnp.concatenate([summed[:mine] + dot(near.astype(BF16), own_values), summed[mine:]], axis=0)
    some = total > 0.0
    safe = jnp.where(some, total, 1.0)
    result = (summed / safe).astype(BF16)
    level = jnp.where(some, top * scale + jnp.log(safe), NEG_BIG)
    first = level.astype(BF16).astype(F32)
    rest = level - first
    second = rest.astype(BF16).astype(F32)
    third = rest - second
    for i in range(4):
        extra = jnp.zeros((RESP, 128), F32)
        for h in range(2):
            at = slice((2 * i + h) * RESP, (2 * i + h + 1) * RESP)
            outs[i][:, h * HEAD_DIM : (h + 1) * HEAD_DIM] = result[at]
            for n, piece in enumerate((first, second, third)):
                extra = jnp.where(lane == 3 * h + n, piece[at], extra)
        outs[i][:, 256:] = extra.astype(BF16)


def attend(info, rows, queries):
    vmem = pl.BlockSpec(memory_space=pltpu.VMEM)
    return pl.pallas_call(
        attend_kernel,
        in_specs=[pl.BlockSpec(memory_space=pltpu.SMEM)] + [vmem] * 5,
        out_shape=(jax.ShapeDtypeStruct((RESP, 384), BF16),) * 4,
        compiler_params=params(SMALL),
        name="attend",
    )(info, rows, *queries)


def merge_kernel(*refs):
    parts, out_ref = refs[:4], refs[4]
    lane = iota((RESP, 128), 1)
    row, col = iota((128, 128), 0), iota((128, 128), 1)
    order = jnp.where(row == by_device(col), 1.0, 0.0).astype(BF16)
    extras = [part[:, 256:].astype(F32) for part in parts]
    for h in range(2):
        head = slice(h * HEAD_DIM, (h + 1) * HEAD_DIM)
        mine = jnp.logical_and(lane >= 3 * h, lane < 3 * h + 3)
        levels = [jnp.sum(jnp.where(mine, e, 0.0), axis=1, keepdims=True) for e in extras]
        top = functools.reduce(jnp.maximum, levels)
        shares = [jnp.exp(level - top) for level in levels]
        total = functools.reduce(jnp.add, shares)
        pieces = [share * part[:, head].astype(F32) for share, part in zip(shares, parts)]
        mean = (functools.reduce(jnp.add, pieces) / total).astype(BF16)
        out_ref[:, head] = dot(mean, order).astype(BF16)


def merge(parts):
    vmem = pl.BlockSpec(memory_space=pltpu.VMEM)
    return pl.pallas_call(
        merge_kernel,
        in_specs=[vmem] * 4,
        out_shape=jax.ShapeDtypeStruct((RESP, 256), BF16),
        compiler_params=params(SMALL),
        name="merge",
    )(*parts)


def z_of(i, info):
    return (4 * info[CORE_AT]) ^ i


def project_own_kernel(info_ref, own_ref, weight_ref, out_ref):
    for i in range(8):
        at = (2 * z_of(i, info_ref) + info_ref[XL_AT]) * BLOCK
        out_ref[i] = dot(own_ref[...], weight_ref[:, pl.ds(pl.multiple_of(at, BLOCK), BLOCK)])


def project_own(info, own, weight):
    vmem = pl.BlockSpec(memory_space=pltpu.VMEM)
    return pl.pallas_call(
        project_own_kernel,
        in_specs=[pl.BlockSpec(memory_space=pltpu.SMEM)] + [vmem] * 2,
        out_shape=jax.ShapeDtypeStruct((8, RESP, BLOCK), F32),
        compiler_params=params(SMALL),
        cost_estimate=LONG,
        name="project_own",
    )(info, own, weight)


def project_kernel(info_ref, started_ref, other_ref, *refs):
    cross, out_ref = refs[:4], refs[4]
    for i in range(8):
        result = started_ref[i] + dot(other_ref[...], cross[i // 2][:, pl.ds((i % 2) * BLOCK, BLOCK)])
        out_ref[z_of(i, info_ref)] = result.astype(BF16)


def project(info, started, other, cross):
    vmem = pl.BlockSpec(memory_space=pltpu.VMEM)
    return pl.pallas_call(
        project_kernel,
        in_specs=[pl.BlockSpec(memory_space=pltpu.SMEM)] + [vmem] * 6,
        out_shape=jax.ShapeDtypeStruct((8, RESP, BLOCK), BF16),
        compiler_params=params(SMALL),
        name="project",
    )(info, started, other, *cross)


def pick_kernel(info_ref, weight_ref, after_ref, *out_refs):
    for i in range(4):
        at = (2 * z_of(i, info_ref) + 1 - info_ref[XL_AT]) * BLOCK
        columns = weight_ref[:, pl.ds(pl.multiple_of(at, BLOCK), BLOCK)]
        out_refs[i // 2][:, (i % 2) * BLOCK : (i % 2) * BLOCK + BLOCK] = columns


def pick_columns(info, weight, after):
    vmem = pl.BlockSpec(memory_space=pltpu.VMEM)
    return pl.pallas_call(
        pick_kernel,
        in_specs=[pl.BlockSpec(memory_space=pltpu.SMEM)] + [vmem] * 2,
        out_shape=(jax.ShapeDtypeStruct((256, 2 * BLOCK), BF16),) * 2,
        compiler_params=params(SMALL),
        name="pick_columns",
    )(info, weight, after)


def swap(values, axis):
    return lax.all_to_all(values, axis, 0, 0, tiled=False)


def body(
    response_hidden,
    prompt_hidden,
    norm_gain,
    query_weight,
    key_weight,
    value_weight,
    output_weight,
    response_lengths,
    prompt_length,
):
    length = prompt_length[0]
    core, y = lax.axis_index("core"), lax.axis_index("y")
    sample, half, xl = lax.axis_index(SAMPLE), lax.axis_index("zl"), lax.axis_index("xl")
    gain = norm_gain.astype(F32).reshape(16, 1, BLOCK)

    row = jnp.arange(ROWS + RESP, dtype=jnp.int32)[:, None]
    lane = jnp.arange(HEAD_DIM, dtype=jnp.int32)[None, :]
    sample_of = sample - core + (lane >> 6)
    positions = jnp.where(
        row < 128,
        sample_of * PROMPT_ROWS + half * 128 + row,
        jnp.where(row < ROWS, length + half * 32 + row - 128, length + row - ROWS),
    )
    entry = (2 * ((lane >> 2) & 7) + xl) * 8 + 4 * core + (lane & 3)
    entry = jnp.where(row < ROWS, entry, lane)
    still = (row < ROWS) & ((lane & 32) > 0)
    inverse = ROPE_BASE ** (-((entry % HALF).astype(F32) * 2.0 / HEAD_DIM))
    angles = jnp.where(still, 0.0, positions.astype(F32) * inverse)
    trig = jnp.stack([jnp.cos(angles), jnp.sin(angles) * jnp.where(entry < HALF, -1.0, 1.0)])

    info = jnp.stack(
        [core, xl, lax.axis_index(TENSOR), y, lax.axis_index(("xh", "core")), length]
    ).astype(jnp.int32)
    flip = [(0, 1), (1, 0)]

    packed = pack(core.reshape(1), key_weight.T, value_weight.T, response_hidden)
    got = swap(packed, ZRING)
    scaled = scale_rows(info, prompt_hidden, response_hidden, gain)
    beside = lax.ppermute(scaled, "xl", flip)
    crossed = lax.ppermute(scaled, "core", flip), lax.ppermute(beside, "core", flip)
    sent = pick_columns(info, output_weight, scaled)
    early, late = (lax.ppermute(piece, "xl", flip) for piece in sent)
    own_hidden = split(got, (*crossed, early, sent[1], trig))
    other_hidden = lax.ppermute(own_hidden, "xl", flip)
    products = partial_products(info, got, (scaled, beside, *crossed))
    products = swap(products, ZRING)
    queries = queries_of(info, gain, query_weight, trig, own_hidden, other_hidden)
    cross = (early, late, lax.ppermute(early, "core", flip), lax.ppermute(late, "core", flip))
    rows = finish_keys(products, trig, queries)
    rows = swap(rows, KEY_GROUP)

    def along(values, step):
        return lax.ppermute(values, "y", [(i, (i + step) % 4) for i in range(4)])

    around = {step: along(queries, step) for step in (2, 1, 3)}
    pooled = [queries] + [around[step] for step in (1, 2, 3)]
    parts = attend(info, rows, pooled)
    attention = merge([along(parts[step], -step) for step in (2, 1, 3)] + [parts[0]])
    partner = lax.ppermute(attention, "xl", flip)
    partial = project(info, project_own(info, attention, output_weight), partner, cross)
    summed = jnp.sum(swap(partial, ZRING).astype(F32), axis=0)
    live = jnp.arange(RESP, dtype=jnp.int32) < response_lengths[0]
    return jnp.where(live[:, None], summed, 0.0).astype(BF16)


def solution(mesh):
    names = tuple(name for name, _ in PARTS)
    sizes = tuple(size for _, size in PARTS)
    fine = Mesh(mesh.devices.reshape(sizes), names)
    return jax.shard_map(
        body,
        mesh=fine,
        in_specs=(
            P(SAMPLE, TENSOR),
            P(SAMPLE, TENSOR),
            P(),
            P(None, TENSOR),
            P(None, TENSOR),
            P(None, TENSOR),
            P(TENSOR, None),
            P(SAMPLE),
            P(),
        ),
        out_specs=P(SAMPLE, TENSOR),
        check_vma=False,
    )
```

```python
import functools
import math

import jax
import jax.numpy as jnp
from jax import lax
from jax.experimental import pallas as pl
from jax.experimental.pallas import tpu as pltpu
from jax.sharding import Mesh
from jax.sharding import PartitionSpec as P

PARTS = (("xh", 2), ("y", 4), ("core", 2), ("k", 4), ("zl", 2), ("xl", 2))
SAMPLE = ("xh", "y", "core")
TENSOR = ("k", "zl", "xl")
ZRING = ("k", "zl")
KEY_GROUP = ("xh", "core", "zl", "xl")

D = 8192
BLOCK = 512
HEAD_DIM = 128
HALF = 64
RESP = 64
PROMPT_ROWS = 256
ROWS = 160
SHARED_ROWS = 144
SENT_ROWS = ROWS + 16
PACKED = 64 + RESP
EPSILON = 1e-05
ROPE_BASE = 500000.0
NEG_BIG = -1e30
CORE_AT, XL_AT, T_AT, Y_AT, PLACE_AT, LENGTH_AT = 0, 1, 2, 3, 4, 5
F32 = jnp.float32
BF16 = jnp.bfloat16
SMALL = 12 * 1024 * 1024


def iota(shape, dim):
    return lax.broadcasted_iota(jnp.int32, shape, dim)


def dot_t(a, b):
    return lax.dot_general(a, b, (((1,), (1,)), ((), ())), preferred_element_type=F32)


def dot(a, b):
    return lax.dot_general(a, b, (((1,), (0,)), ((), ())), preferred_element_type=F32)


LONG = pl.CostEstimate(flops=30_000_000_000, bytes_accessed=1_000_000, transcendentals=0)


def params(limit=None):
    return pltpu.CompilerParams(vmem_limit_bytes=limit)


def pack_kernel(core_ref, key_ref, value_ref, hidden_ref, out_ref):
    for i in range(out_ref.shape[0]):
        for x in range(2):
            at = (2 * i + x) * BLOCK
            out_ref[i, 32 * x : 32 * x + 16] = key_ref[:, at : at + BLOCK]
            out_ref[i, 32 * x + 16 : 32 * x + 32] = value_ref[:, at : at + BLOCK]
        out_ref[i, 64:] = hidden_ref[...]


def pack(core, key_rows, value_rows, hidden):
    steps = 2
    each = 8 // steps
    rows = pl.BlockSpec((16, 2 * each * BLOCK), lambda i, core: (core[0], i))
    return pl.pallas_call(
        pack_kernel,
        grid_spec=pltpu.PrefetchScalarGridSpec(
            num_scalar_prefetch=1,
            grid=(steps,),
            in_specs=[rows, rows, pl.BlockSpec((RESP, BLOCK), lambda i, core: (0, 0))],
            out_specs=pl.BlockSpec((each, PACKED, BLOCK), lambda i, core: (i, 0, 0)),
        ),
        out_shape=jax.ShapeDtypeStruct((8, PACKED, BLOCK), BF16),
        compiler_params=params(),
        name="pack",
    )(core, key_rows, value_rows, hidden)


def scale_kernel(info_ref, prompt_ref, resp_ref, gain_ref, out_ref, high, low):
    gain = gain_ref[info_ref[T_AT]]

    def put(at, count, values):
        values = values.astype(F32)
        out_ref[at : at + count] = (values * gain).astype(BF16)
        square = values * values
        top = square.astype(BF16)
        high[at : at + count] = top
        low[at : at + count] = (square - top.astype(F32)).astype(BF16)

    for half in range(2):
        put(ROWS * half, 128, prompt_ref[128 * half : 128 * half + 128])
        put(ROWS * half + 128, 32, resp_ref[32 * half : 32 * half + 32])
    high[320:448] = jnp.zeros((128, BLOCK), BF16)
    low[320:448] = jnp.zeros((128, BLOCK), BF16)
    ones = jnp.ones((16, BLOCK), BF16)
    row = iota((16, 128), 0)
    rows = jnp.zeros((16, 128), F32)
    for n, at in enumerate((0, 128, ROWS, ROWS + 128)):
        total = dot_t(ones, high[at : at + 128]) + dot_t(ones, low[at : at + 128])
        top = total.astype(BF16).astype(F32)
        rows = jnp.where(row == 2 * n, top, jnp.where(row == 2 * n + 1, total - top, rows))
    out_ref[320:, :128] = rows.astype(BF16)
    out_ref[320:, 128:] = jnp.zeros((16, BLOCK - 128), BF16)


def scale_rows(info, prompt, resp, gain):
    vmem = pl.BlockSpec(memory_space=pltpu.VMEM)
    return pl.pallas_call(
        scale_kernel,
        in_specs=[pl.BlockSpec(memory_space=pltpu.SMEM), vmem, vmem, vmem],
        out_shape=jax.ShapeDtypeStruct((2 * ROWS + 16, BLOCK), BF16),
        scratch_shapes=[pltpu.VMEM((448, BLOCK), BF16), pltpu.VMEM((448, BLOCK), BF16)],
        compiler_params=params(SMALL),
        name="scale_rows",
    )(info, prompt, resp, gain)


def split_kernel(got_ref, *refs):
    refs[-1][...] = got_ref[:, 64:]


def split(got, after):
    return pl.pallas_call(
        split_kernel,
        in_specs=[pl.BlockSpec(memory_space=pltpu.VMEM)] * (1 + len(after)),
        out_shape=jax.ShapeDtypeStruct((8, RESP, BLOCK), BF16),
        compiler_params=params(SMALL),
        name="split",
    )(got, *after)


def partial_kernel(info_ref, got_ref, *refs):
    out_ref = refs[4]
    xl, core = info_ref[XL_AT], info_ref[CORE_AT]
    weights = [got_ref[:, pl.ds(pl.multiple_of(32 * x, 32), 32)].reshape(256, BLOCK) for x in (xl, 1 - xl)]
    row, col = iota((256, 512), 0), iota((256, 512), 1)
    target = (row & 3) * 128 + (row >> 5) * 8 + ((row >> 2) & 7)
    total = jnp.zeros((2 * ROWS, 512), F32)
    sums = []
    for n, at in enumerate((core, 1 - core)):
        here, there = refs[2 * n], refs[2 * n + 1]
        raw = dot_t(here[: 2 * ROWS], weights[0]) + dot_t(there[: 2 * ROWS], weights[1])
        pick = jnp.where(col == target + 64 * at, 1.0, 0.0).astype(BF16)
        total += dot(raw.astype(BF16), pick)
        sums.append((here[2 * ROWS :, :128], there[2 * ROWS :, :128]))
    total = total.astype(BF16)
    for half in range(2):
        lines = [[piece[4 * half : 4 * half + 4] for piece in pair] for pair in sums]
        lines = [jnp.concatenate(lines[0] + lines[1], axis=0), jnp.concatenate(lines[1] + lines[0], axis=0)]
        for head in range(4):
            to = 2 * head + half
            out_ref[to, :ROWS] = total[ROWS * half : ROWS * half + ROWS, head * 128 : head * 128 + 128]
            out_ref[to, ROWS:] = jnp.where(core == 0, lines[0], lines[1])


def partial_products(info, got, blocks):
    vmem = pl.BlockSpec(memory_space=pltpu.VMEM)
    return pl.pallas_call(
        partial_kernel,
        in_specs=[pl.BlockSpec(memory_space=pltpu.SMEM)] + [vmem] * 5,
        out_shape=jax.ShapeDtypeStruct((8, SENT_ROWS, 128), BF16),
        compiler_params=params(SMALL),
        name="partial_products",
    )(info, got, *blocks)


def turn(values, cosine, sine):
    return values * cosine + pltpu.roll(values, HALF, 1) * sine


def finish_kernel(parts_ref, trig_ref, *refs):
    out_ref = refs[-1]
    total = jnp.sum(parts_ref[...].astype(F32), axis=0)
    sums = total[ROWS:]
    factors = []
    for core in range(2):
        column = []
        for n, count in enumerate((128, ROWS - 128)):
            at = 8 * core + 2 * n
            line = sums[at : at + 1] + sums[at + 1 : at + 2] + sums[at + 4 : at + 5] + sums[at + 5 : at + 6]
            diagonal = iota((count, 128), 0) == iota((count, 128), 1)
            spread = jnp.where(diagonal, jnp.broadcast_to(line, (count, 128)), 0.0)
            column.append(jnp.sum(spread, axis=1, keepdims=True))
        factors.append(lax.rsqrt(jnp.concatenate(column, axis=0) * (1.0 / D) + EPSILON))
    factor = jnp.where(iota((ROWS, 128), 1) < 64, factors[0], factors[1])
    raw = (total[:ROWS] * factor).astype(BF16)
    row, col = iota((128, 128), 0), iota((128, 128), 1)
    target = (row & 64) + ((row >> 2) & 1) * 32 + ((row >> 3) & 7) * 4 + (row & 3)
    ordered = dot(raw, jnp.where(col == target, 1.0, 0.0).astype(BF16))
    beside = dot(raw, jnp.where(col == (target ^ 16), 1.0, 0.0).astype(BF16))
    result = ordered * trig_ref[0, :ROWS] + beside * trig_ref[1, :ROWS]
    prompt = result[:128].astype(BF16)
    first, second = result[128:144], result[144:160]
    left = iota((16, 128), 1) < 64
    resp = (
        jnp.where(left, first, pltpu.roll(second, 64, 1)).astype(BF16),
        jnp.where(left, pltpu.roll(first, 64, 1), second).astype(BF16),
    )
    for i in range(out_ref.shape[0]):
        out_ref[i, :128] = prompt
        out_ref[i, 128:] = resp[(i >> 2) & 1]


def finish_keys(parts, trig, *after):
    return pl.pallas_call(
        finish_kernel,
        in_specs=[pl.BlockSpec(memory_space=pltpu.VMEM)] * (2 + len(after)),
        out_shape=jax.ShapeDtypeStruct((16, SHARED_ROWS, 128), BF16),
        compiler_params=params(SMALL),
        cost_estimate=LONG,
        name="finish_keys",
    )(parts, trig, *after)


def by_device(natural):
    return ((natural >> 3) & 1) * 64 + ((natural >> 2) & 1) * 32 + (natural >> 4) * 4 + (natural & 3)


def query_kernel(info_ref, gain_ref, trig_ref, weight_ref, own_ref, other_ref, out_ref):
    xl = info_ref[XL_AT]
    total = jnp.zeros((RESP, 256), F32)
    squares = jnp.zeros((RESP, 1), F32)
    for z in range(8):
        for j, ref in enumerate((own_ref, other_ref)):
            x = j ^ xl
            hidden = ref[z].astype(F32)
            scaled = (hidden * gain_ref[2 * z + x]).astype(BF16)
            total += dot(scaled, weight_ref[pl.ds(pl.multiple_of((2 * z + x) * BLOCK, BLOCK), BLOCK)])
            squares += jnp.sum(hidden * hidden, axis=1, keepdims=True)
    factor = lax.rsqrt(squares * (1.0 / D) + EPSILON)
    row, col = iota((128, 128), 0), iota((128, 128), 1)
    order = jnp.where(col == by_device(row), 1.0, 0.0).astype(BF16)
    for h in range(2):
        part = slice(h * HEAD_DIM, (h + 1) * HEAD_DIM)
        query = turn(total[:, part] * factor, trig_ref[0, ROWS:], trig_ref[1, ROWS:])
        out_ref[:, part] = dot(query.astype(BF16), order).astype(BF16)


def queries_of(info, gain, weight, trig, own, other):
    vmem = pl.BlockSpec(memory_space=pltpu.VMEM)
    return pl.pallas_call(
        query_kernel,
        in_specs=[pl.BlockSpec(memory_space=pltpu.SMEM)] + [vmem] * 5,
        out_shape=jax.ShapeDtypeStruct((RESP, 256), BF16),
        compiler_params=params(SMALL),
        cost_estimate=LONG,
        name="queries",
    )(info, gain, trig, weight, own, other)


def attend_kernel(info_ref, rows_ref, *refs):
    queries, outs = refs[:4], refs[4:]
    own_y = info_ref[Y_AT]

    def joined(xh, zl, at, count):
        group = iota((count, 128), 1) >> 5
        pieces = [
            rows_ref[xh * 8 + core * 4 + zl * 2 + x, at : at + count].astype(F32) for x in range(2) for core in range(2)
        ]
        result = []
        for g in range(4):
            rows = pltpu.roll(pieces[0], (-32 * g) % 128, 1) if g else pieces[0]
            for p in range(1, 4):
                shift = (32 * (p - g)) % 128
                rows = jnp.where(group == p, pltpu.roll(pieces[p], shift, 1) if shift else pieces[p], rows)
            result.append(rows.astype(BF16))
        return result

    prompt = [[joined(xh, zl, 0, 128) for zl in range(2)] for xh in range(2)]

    def prompt_rows(kv):
        return jnp.concatenate(
            [prompt[xh][zl][2 * core + kv] for xh in range(2) for core in range(2) for zl in range(2)], axis=0
        )

    prompt_keys, prompt_values = prompt_rows(0), prompt_rows(1)
    own_xh = info_ref[PLACE_AT] // 2
    own = [joined(own_xh, zl, 128, 16) for zl in range(2)]

    def own_rows(kv):
        return jnp.concatenate([o[2 * n + kv] for o in own for n in range(2)], axis=0)

    own_keys, own_values = own_rows(0), own_rows(1)
    scale = HEAD_DIM ** (-0.5)
    power = scale * math.log2(math.e)

    column = iota((1, 1024), 1)
    sample = (column >> 9) * 8 + own_y * 2 + ((column >> 8) & 1)
    live = sample * PROMPT_ROWS + (column & 255) < info_ref[LENGTH_AT]
    causal = iota((2 * RESP, RESP), 1) <= (iota((2 * RESP, RESP), 0) & (RESP - 1))
    lane = iota((RESP, 128), 1)

    query = jnp.concatenate([q[:, h * HEAD_DIM : (h + 1) * HEAD_DIM] for q in queries for h in range(2)], axis=0)
    mine = 2 * RESP
    far = jnp.where(live, dot_t(query, prompt_keys), NEG_BIG)
    near = jnp.where(causal, dot_t(query[:mine], own_keys), NEG_BIG)
    top = jnp.max(far, axis=1, keepdims=True)
    top_mine = jnp.maximum(top[:mine], jnp.max(near, axis=1, keepdims=True))
    top = jnp.maximum(jnp.concatenate([top_mine, top[mine:]], axis=0), 0.5 * NEG_BIG)
    far = jnp.exp2((far - top) * power)
    near = jnp.exp2((near - top[:mine]) * power)
    total = jnp.sum(far, axis=1, keepdims=True)
    total = jnp.concatenate([total[:mine] + jnp.sum(near, axis=1, keepdims=True), total[mine:]], axis=0)
    summed = dot(far.astype(BF16), prompt_values)
    summed = jnp.concatenate([summed[:mine] + dot(near.astype(BF16), own_values), summed[mine:]], axis=0)
    some = total > 0.0
    safe = jnp.where(some, total, 1.0)
    result = (summed / safe).astype(BF16)
    level = jnp.where(some, top * scale + jnp.log(safe), NEG_BIG)
    first = level.astype(BF16).astype(F32)
    rest = level - first
    second = rest.astype(BF16).astype(F32)
    third = rest - second
    for i in range(4):
        extra = jnp.zeros((RESP, 128), F32)
        for h in range(2):
            at = slice((2 * i + h) * RESP, (2 * i + h + 1) * RESP)
            outs[i][:, h * HEAD_DIM : (h + 1) * HEAD_DIM] = result[at]
            for n, piece in enumerate((first, second, third)):
                extra = jnp.where(lane == 3 * h + n, piece[at], extra)
        outs[i][:, 256:] = extra.astype(BF16)


def attend(info, rows, queries):
    vmem = pl.BlockSpec(memory_space=pltpu.VMEM)
    return pl.pallas_call(
        attend_kernel,
        in_specs=[pl.BlockSpec(memory_space=pltpu.SMEM)] + [vmem] * 5,
        out_shape=(jax.ShapeDtypeStruct((RESP, 384), BF16),) * 4,
        compiler_params=params(SMALL),
        name="attend",
    )(info, rows, *queries)


def merge_kernel(*refs):
    parts, out_ref = refs[:4], refs[-1]
    lane = iota((RESP, 128), 1)
    row, col = iota((128, 128), 0), iota((128, 128), 1)
    order = jnp.where(row == by_device(col), 1.0, 0.0).astype(BF16)
    extras = [part[:, 256:].astype(F32) for part in parts]
    for h in range(2):
        head = slice(h * HEAD_DIM, (h + 1) * HEAD_DIM)
        mine = jnp.logical_and(lane >= 3 * h, lane < 3 * h + 3)
        levels = [jnp.sum(jnp.where(mine, e, 0.0), axis=1, keepdims=True) for e in extras]
        top = functools.reduce(jnp.maximum, levels)
        shares = [jnp.exp(level - top) for level in levels]
        total = functools.reduce(jnp.add, shares)
        pieces = [share * part[:, head].astype(F32) for share, part in zip(shares, parts)]
        mean = (functools.reduce(jnp.add, pieces) / total).astype(BF16)
        out_ref[:, head] = dot(mean, order).astype(BF16)


def merge(parts, after):
    vmem = pl.BlockSpec(memory_space=pltpu.VMEM)
    return pl.pallas_call(
        merge_kernel,
        in_specs=[vmem] * 5,
        out_shape=jax.ShapeDtypeStruct((RESP, 256), BF16),
        compiler_params=params(SMALL),
        name="merge",
    )(*parts, after)


def z_of(i, info):
    return (4 * info[CORE_AT]) ^ i


def near_kernel(info_ref, weight_ref, after_ref, *out_refs):
    for i in range(8):
        at = (2 * z_of(i, info_ref) + info_ref[XL_AT]) * BLOCK
        columns = weight_ref[:, pl.ds(pl.multiple_of(at, BLOCK), BLOCK)]
        out_refs[i // 2][:, (i % 2) * BLOCK : (i % 2) * BLOCK + BLOCK] = columns


def near_columns(info, weight, after):
    vmem = pl.BlockSpec(memory_space=pltpu.VMEM)
    return pl.pallas_call(
        near_kernel,
        in_specs=[pl.BlockSpec(memory_space=pltpu.SMEM)] + [vmem] * 2,
        out_shape=(jax.ShapeDtypeStruct((256, 2 * BLOCK), BF16),) * 4,
        compiler_params=params(SMALL),
        cost_estimate=LONG,
        name="near_columns",
    )(info, weight, after)


def project_own_kernel(own_ref, *refs):
    weights, out_ref = refs[:4], refs[4]
    for i in range(8):
        out_ref[i] = dot(own_ref[...], weights[i // 2][:, pl.ds((i % 2) * BLOCK, BLOCK)])


def project_own(own, weights):
    vmem = pl.BlockSpec(memory_space=pltpu.VMEM)
    return pl.pallas_call(
        project_own_kernel,
        in_specs=[vmem] * 5,
        out_shape=jax.ShapeDtypeStruct((8, RESP, BLOCK), F32),
        compiler_params=params(SMALL),
        cost_estimate=LONG,
        name="project_own",
    )(own, *weights)


def project_kernel(info_ref, started_ref, other_ref, *refs):
    cross, out_ref = refs[:4], refs[4]
    for i in range(8):
        result = started_ref[i] + dot(other_ref[...], cross[i // 2][:, pl.ds((i % 2) * BLOCK, BLOCK)])
        out_ref[z_of(i, info_ref)] = result.astype(BF16)


def project(info, started, other, cross):
    vmem = pl.BlockSpec(memory_space=pltpu.VMEM)
    return pl.pallas_call(
        project_kernel,
        in_specs=[pl.BlockSpec(memory_space=pltpu.SMEM)] + [vmem] * 6,
        out_shape=jax.ShapeDtypeStruct((8, RESP, BLOCK), BF16),
        compiler_params=params(SMALL),
        name="project",
    )(info, started, other, *cross)


def pick_kernel(info_ref, weight_ref, after_ref, *out_refs):
    for i in range(4):
        at = (2 * z_of(i, info_ref) + 1 - info_ref[XL_AT]) * BLOCK
        columns = weight_ref[:, pl.ds(pl.multiple_of(at, BLOCK), BLOCK)]
        out_refs[i // 2][:, (i % 2) * BLOCK : (i % 2) * BLOCK + BLOCK] = columns


def pick_columns(info, weight, after):
    vmem = pl.BlockSpec(memory_space=pltpu.VMEM)
    return pl.pallas_call(
        pick_kernel,
        in_specs=[pl.BlockSpec(memory_space=pltpu.SMEM)] + [vmem] * 2,
        out_shape=(jax.ShapeDtypeStruct((256, 2 * BLOCK), BF16),) * 2,
        compiler_params=params(SMALL),
        name="pick_columns",
    )(info, weight, after)


def swap(values, axis):
    return lax.all_to_all(values, axis, 0, 0, tiled=False)


def body(
    response_hidden,
    prompt_hidden,
    norm_gain,
    query_weight,
    key_weight,
    value_weight,
    output_weight,
    response_lengths,
    prompt_length,
):
    length = prompt_length[0]
    core, y = lax.axis_index("core"), lax.axis_index("y")
    sample, half, xl = lax.axis_index(SAMPLE), lax.axis_index("zl"), lax.axis_index("xl")
    gain = norm_gain.astype(F32).reshape(16, 1, BLOCK)

    row = jnp.arange(ROWS + RESP, dtype=jnp.int32)[:, None]
    lane = jnp.arange(HEAD_DIM, dtype=jnp.int32)[None, :]
    sample_of = sample - core + (lane >> 6)
    positions = jnp.where(
        row < 128,
        sample_of * PROMPT_ROWS + half * 128 + row,
        jnp.where(row < ROWS, length + half * 32 + row - 128, length + row - ROWS),
    )
    entry = (2 * ((lane >> 2) & 7) + xl) * 8 + 4 * core + (lane & 3)
    entry = jnp.where(row < ROWS, entry, lane)
    still = (row < ROWS) & ((lane & 32) > 0)
    inverse = ROPE_BASE ** (-((entry % HALF).astype(F32) * 2.0 / HEAD_DIM))
    angles = jnp.where(still, 0.0, positions.astype(F32) * inverse)
    trig = jnp.stack([jnp.cos(angles), jnp.sin(angles) * jnp.where(entry < HALF, -1.0, 1.0)])

    info = jnp.stack(
        [core, xl, lax.axis_index(TENSOR), y, lax.axis_index(("xh", "core")), length]
    ).astype(jnp.int32)
    flip = [(0, 1), (1, 0)]

    packed = pack(core.reshape(1), key_weight.T, value_weight.T, response_hidden)
    got = swap(packed, ZRING)
    scaled = scale_rows(info, prompt_hidden, response_hidden, gain)
    beside = lax.ppermute(scaled, "xl", flip)
    crossed = lax.ppermute(scaled, "core", flip), lax.ppermute(beside, "core", flip)
    sent = pick_columns(info, output_weight, scaled)
    early, late = (lax.ppermute(piece, "xl", flip) for piece in sent)
    own_hidden = split(got, (*crossed, early, sent[1], trig))
    other_hidden = lax.ppermute(own_hidden, "xl", flip)
    products = partial_products(info, got, (scaled, beside, *crossed))
    products = swap(products, ZRING)
    queries = queries_of(info, gain, query_weight, trig, own_hidden, other_hidden)
    cross = (early, late, lax.ppermute(early, "core", flip), lax.ppermute(late, "core", flip))
    rows = finish_keys(products, trig, queries)
    rows = swap(rows, KEY_GROUP)

    def along(values, step):
        return lax.ppermute(values, "y", [(i, (i + step) % 4) for i in range(4)])

    pooled = [queries] + [along(queries, step) for step in (1, 2, 3)]
    parts = attend(info, rows, pooled)
    near = near_columns(info, output_weight, parts[0])
    attention = merge([parts[0]] + [along(parts[step], -step) for step in (1, 2, 3)], near[0])
    partner = lax.ppermute(attention, "xl", flip)
    partial = project(info, project_own(attention, near), partner, cross)
    summed = jnp.sum(swap(partial, ZRING).astype(F32), axis=0)
    live = jnp.arange(RESP, dtype=jnp.int32) < response_lengths[0]
    return jnp.where(live[:, None], summed, 0.0).astype(BF16)


def solution(mesh):
    names = tuple(name for name, _ in PARTS)
    sizes = tuple(size for _, size in PARTS)
    fine = Mesh(mesh.devices.reshape(sizes), names)
    return jax.shard_map(
        body,
        mesh=fine,
        in_specs=(
            P(SAMPLE, TENSOR),
            P(SAMPLE, TENSOR),
            P(),
            P(None, TENSOR),
            P(None, TENSOR),
            P(None, TENSOR),
            P(TENSOR, None),
            P(SAMPLE),
            P(),
        ),
        out_specs=P(SAMPLE, TENSOR),
        check_vma=False,
    )
```

```python
import functools
import math

import jax
import jax.numpy as jnp
from jax import lax
from jax.experimental import pallas as pl
from jax.experimental.pallas import tpu as pltpu
from jax.sharding import Mesh
from jax.sharding import PartitionSpec as P

PARTS = (("xh", 2), ("y", 4), ("core", 2), ("k", 4), ("zl", 2), ("xl", 2))
SAMPLE = ("xh", "y", "core")
TENSOR = ("k", "zl", "xl")
ZRING = ("k", "zl")
KEY_GROUP = ("xh", "core", "zl", "xl")

D = 8192
BLOCK = 512
HEAD_DIM = 128
HALF = 64
RESP = 64
PROMPT_ROWS = 256
ROWS = 160
SHARED_ROWS = 144
SENT_ROWS = ROWS + 16
PACKED = 64 + RESP
EPSILON = 1e-05
ROPE_BASE = 500000.0
NEG_BIG = -1e30
CORE_AT, XL_AT, T_AT, Y_AT, PLACE_AT, LENGTH_AT = 0, 1, 2, 3, 4, 5
F32 = jnp.float32
BF16 = jnp.bfloat16
SMALL = 12 * 1024 * 1024


def iota(shape, dim):
    return lax.broadcasted_iota(jnp.int32, shape, dim)


def dot_t(a, b):
    return lax.dot_general(a, b, (((1,), (1,)), ((), ())), preferred_element_type=F32)


def dot(a, b):
    return lax.dot_general(a, b, (((1,), (0,)), ((), ())), preferred_element_type=F32)


LONG = pl.CostEstimate(flops=30_000_000_000, bytes_accessed=1_000_000, transcendentals=0)


def params(limit=None):
    return pltpu.CompilerParams(vmem_limit_bytes=limit)


def pack_kernel(core_ref, key_ref, value_ref, hidden_ref, out_ref):
    for i in range(out_ref.shape[0]):
        for x in range(2):
            at = (2 * i + x) * BLOCK
            out_ref[i, 32 * x : 32 * x + 16] = key_ref[:, at : at + BLOCK]
            out_ref[i, 32 * x + 16 : 32 * x + 32] = value_ref[:, at : at + BLOCK]
        out_ref[i, 64:] = hidden_ref[...]


def pack(core, key_rows, value_rows, hidden):
    steps = 2
    each = 8 // steps
    rows = pl.BlockSpec((16, 2 * each * BLOCK), lambda i, core: (core[0], i))
    return pl.pallas_call(
        pack_kernel,
        grid_spec=pltpu.PrefetchScalarGridSpec(
            num_scalar_prefetch=1,
            grid=(steps,),
            in_specs=[rows, rows, pl.BlockSpec((RESP, BLOCK), lambda i, core: (0, 0))],
            out_specs=pl.BlockSpec((each, PACKED, BLOCK), lambda i, core: (i, 0, 0)),
        ),
        out_shape=jax.ShapeDtypeStruct((8, PACKED, BLOCK), BF16),
        compiler_params=params(),
        name="pack",
    )(core, key_rows, value_rows, hidden)


def scale_kernel(info_ref, prompt_ref, resp_ref, gain_ref, out_ref, high, low):
    gain = gain_ref[info_ref[T_AT]]

    def put(at, count, values):
        values = values.astype(F32)
        out_ref[at : at + count] = (values * gain).astype(BF16)
        square = values * values
        top = square.astype(BF16)
        high[at : at + count] = top
        low[at : at + count] = (square - top.astype(F32)).astype(BF16)

    for half in range(2):
        put(ROWS * half, 128, prompt_ref[128 * half : 128 * half + 128])
        put(ROWS * half + 128, 32, resp_ref[32 * half : 32 * half + 32])
    high[320:448] = jnp.zeros((128, BLOCK), BF16)
    low[320:448] = jnp.zeros((128, BLOCK), BF16)
    ones = jnp.ones((16, BLOCK), BF16)
    row = iota((16, 128), 0)
    rows = jnp.zeros((16, 128), F32)
    for n, at in enumerate((0, 128, ROWS, ROWS + 128)):
        total = dot_t(ones, high[at : at + 128]) + dot_t(ones, low[at : at + 128])
        top = total.astype(BF16).astype(F32)
        rows = jnp.where(row == 2 * n, top, jnp.where(row == 2 * n + 1, total - top, rows))
    out_ref[320:, :128] = rows.astype(BF16)
    out_ref[320:, 128:] = jnp.zeros((16, BLOCK - 128), BF16)


def scale_rows(info, prompt, resp, gain):
    vmem = pl.BlockSpec(memory_space=pltpu.VMEM)
    return pl.pallas_call(
        scale_kernel,
        in_specs=[pl.BlockSpec(memory_space=pltpu.SMEM), vmem, vmem, vmem],
        out_shape=jax.ShapeDtypeStruct((2 * ROWS + 16, BLOCK), BF16),
        scratch_shapes=[pltpu.VMEM((448, BLOCK), BF16), pltpu.VMEM((448, BLOCK), BF16)],
        compiler_params=params(SMALL),
        name="scale_rows",
    )(info, prompt, resp, gain)


def split_kernel(got_ref, *refs):
    refs[-1][...] = got_ref[:, 64:]


def split(got, after):
    return pl.pallas_call(
        split_kernel,
        in_specs=[pl.BlockSpec(memory_space=pltpu.VMEM)] * (1 + len(after)),
        out_shape=jax.ShapeDtypeStruct((8, RESP, BLOCK), BF16),
        compiler_params=params(SMALL),
        name="split",
    )(got, *after)


def partial_kernel(info_ref, got_ref, *refs):
    out_ref = refs[4]
    xl, core = info_ref[XL_AT], info_ref[CORE_AT]
    weights = [got_ref[:, pl.ds(pl.multiple_of(32 * x, 32), 32)].reshape(256, BLOCK) for x in (xl, 1 - xl)]
    row, col = iota((256, 512), 0), iota((256, 512), 1)
    target = (row & 3) * 128 + (row >> 5) * 8 + ((row >> 2) & 7)
    total = jnp.zeros((2 * ROWS, 512), F32)
    sums = []
    for n, at in enumerate((core, 1 - core)):
        here, there = refs[2 * n], refs[2 * n + 1]
        raw = dot_t(here[: 2 * ROWS], weights[0]) + dot_t(there[: 2 * ROWS], weights[1])
        pick = jnp.where(col == target + 64 * at, 1.0, 0.0).astype(BF16)
        total += dot(raw.astype(BF16), pick)
        sums.append((here[2 * ROWS :, :128], there[2 * ROWS :, :128]))
    total = total.astype(BF16)
    for half in range(2):
        lines = [[piece[4 * half : 4 * half + 4] for piece in pair] for pair in sums]
        lines = [jnp.concatenate(lines[0] + lines[1], axis=0), jnp.concatenate(lines[1] + lines[0], axis=0)]
        for head in range(4):
            to = 2 * head + half
            out_ref[to, :ROWS] = total[ROWS * half : ROWS * half + ROWS, head * 128 : head * 128 + 128]
            out_ref[to, ROWS:] = jnp.where(core == 0, lines[0], lines[1])


def partial_products(info, got, blocks):
    vmem = pl.BlockSpec(memory_space=pltpu.VMEM)
    return pl.pallas_call(
        partial_kernel,
        in_specs=[pl.BlockSpec(memory_space=pltpu.SMEM)] + [vmem] * 5,
        out_shape=jax.ShapeDtypeStruct((8, SENT_ROWS, 128), BF16),
        compiler_params=params(SMALL),
        name="partial_products",
    )(info, got, *blocks)


def turn(values, cosine, sine):
    return values * cosine + pltpu.roll(values, HALF, 1) * sine


def finish_kernel(parts_ref, trig_ref, *refs):
    out_ref = refs[-1]
    total = jnp.sum(parts_ref[...].astype(F32), axis=0)
    sums = total[ROWS:]
    factors = []
    for core in range(2):
        column = []
        for n, count in enumerate((128, ROWS - 128)):
            at = 8 * core + 2 * n
            line = sums[at : at + 1] + sums[at + 1 : at + 2] + sums[at + 4 : at + 5] + sums[at + 5 : at + 6]
            diagonal = iota((count, 128), 0) == iota((count, 128), 1)
            spread = jnp.where(diagonal, jnp.broadcast_to(line, (count, 128)), 0.0)
            column.append(jnp.sum(spread, axis=1, keepdims=True))
        factors.append(lax.rsqrt(jnp.concatenate(column, axis=0) * (1.0 / D) + EPSILON))
    factor = jnp.where(iota((ROWS, 128), 1) < 64, factors[0], factors[1])
    raw = (total[:ROWS] * factor).astype(BF16)
    row, col = iota((128, 128), 0), iota((128, 128), 1)
    target = (row & 64) + ((row >> 2) & 1) * 32 + ((row >> 3) & 7) * 4 + (row & 3)
    ordered = dot(raw, jnp.where(col == target, 1.0, 0.0).astype(BF16))
    beside = dot(raw, jnp.where(col == (target ^ 16), 1.0, 0.0).astype(BF16))
    result = ordered * trig_ref[0, :ROWS] + beside * trig_ref[1, :ROWS]
    prompt = result[:128].astype(BF16)
    first, second = result[128:144], result[144:160]
    left = iota((16, 128), 1) < 64
    resp = (
        jnp.where(left, first, pltpu.roll(second, 64, 1)).astype(BF16),
        jnp.where(left, pltpu.roll(first, 64, 1), second).astype(BF16),
    )
    for i in range(out_ref.shape[0]):
        out_ref[i, :128] = prompt
        out_ref[i, 128:] = resp[(i >> 2) & 1]


def finish_keys(parts, trig, *after):
    return pl.pallas_call(
        finish_kernel,
        in_specs=[pl.BlockSpec(memory_space=pltpu.VMEM)] * (2 + len(after)),
        out_shape=jax.ShapeDtypeStruct((16, SHARED_ROWS, 128), BF16),
        compiler_params=params(SMALL),
        cost_estimate=LONG,
        name="finish_keys",
    )(parts, trig, *after)


def by_device(natural):
    return ((natural >> 3) & 1) * 64 + ((natural >> 2) & 1) * 32 + (natural >> 4) * 4 + (natural & 3)


def query_kernel(info_ref, gain_ref, trig_ref, weight_ref, own_ref, other_ref, out_ref):
    xl = info_ref[XL_AT]
    total = jnp.zeros((RESP, 256), F32)
    squares = jnp.zeros((RESP, 1), F32)
    for z in range(8):
        for j, ref in enumerate((own_ref, other_ref)):
            x = j ^ xl
            hidden = ref[z].astype(F32)
            scaled = (hidden * gain_ref[2 * z + x]).astype(BF16)
            total += dot(scaled, weight_ref[pl.ds(pl.multiple_of((2 * z + x) * BLOCK, BLOCK), BLOCK)])
            squares += jnp.sum(hidden * hidden, axis=1, keepdims=True)
    factor = lax.rsqrt(squares * (1.0 / D) + EPSILON)
    row, col = iota((128, 128), 0), iota((128, 128), 1)
    order = jnp.where(col == by_device(row), 1.0, 0.0).astype(BF16)
    for h in range(2):
        part = slice(h * HEAD_DIM, (h + 1) * HEAD_DIM)
        query = turn(total[:, part] * factor, trig_ref[0, ROWS:], trig_ref[1, ROWS:])
        out_ref[:, part] = dot(query.astype(BF16), order).astype(BF16)


def queries_of(info, gain, weight, trig, own, other):
    vmem = pl.BlockSpec(memory_space=pltpu.VMEM)
    return pl.pallas_call(
        query_kernel,
        in_specs=[pl.BlockSpec(memory_space=pltpu.SMEM)] + [vmem] * 5,
        out_shape=jax.ShapeDtypeStruct((RESP, 256), BF16),
        compiler_params=params(SMALL),
        cost_estimate=LONG,
        name="queries",
    )(info, gain, trig, weight, own, other)


def attend_kernel(info_ref, rows_ref, *refs):
    queries, outs = refs[:4], refs[4:]
    own_y = info_ref[Y_AT]

    def joined(xh, zl, at, count):
        group = iota((count, 128), 1) >> 5
        pieces = [
            rows_ref[xh * 8 + core * 4 + zl * 2 + x, at : at + count].astype(F32) for x in range(2) for core in range(2)
        ]
        result = []
        for g in range(4):
            rows = pltpu.roll(pieces[0], (-32 * g) % 128, 1) if g else pieces[0]
            for p in range(1, 4):
                shift = (32 * (p - g)) % 128
                rows = jnp.where(group == p, pltpu.roll(pieces[p], shift, 1) if shift else pieces[p], rows)
            result.append(rows.astype(BF16))
        return result

    prompt = [[joined(xh, zl, 0, 128) for zl in range(2)] for xh in range(2)]

    def prompt_rows(kv):
        return jnp.concatenate(
            [prompt[xh][zl][2 * core + kv] for xh in range(2) for core in range(2) for zl in range(2)], axis=0
        )

    prompt_keys, prompt_values = prompt_rows(0), prompt_rows(1)
    own_xh = info_ref[PLACE_AT] // 2
    own = [joined(own_xh, zl, 128, 16) for zl in range(2)]

    def own_rows(kv):
        return jnp.concatenate([o[2 * n + kv] for o in own for n in range(2)], axis=0)

    own_keys, own_values = own_rows(0), own_rows(1)
    scale = HEAD_DIM ** (-0.5)
    power = scale * math.log2(math.e)

    column = iota((1, 1024), 1)
    sample = (column >> 9) * 8 + own_y * 2 + ((column >> 8) & 1)
    live = sample * PROMPT_ROWS + (column & 255) < info_ref[LENGTH_AT]
    causal = iota((2 * RESP, RESP), 1) <= (iota((2 * RESP, RESP), 0) & (RESP - 1))
    lane = iota((RESP, 128), 1)

    query = jnp.concatenate([q[:, h * HEAD_DIM : (h + 1) * HEAD_DIM] for q in queries for h in range(2)], axis=0)
    mine = 2 * RESP
    far = jnp.where(live, dot_t(query, prompt_keys), NEG_BIG)
    near = jnp.where(causal, dot_t(query[:mine], own_keys), NEG_BIG)
    top = jnp.max(far, axis=1, keepdims=True)
    top_mine = jnp.maximum(top[:mine], jnp.max(near, axis=1, keepdims=True))
    top = jnp.maximum(jnp.concatenate([top_mine, top[mine:]], axis=0), 0.5 * NEG_BIG)
    far = jnp.exp2((far - top) * power)
    near = jnp.exp2((near - top[:mine]) * power)
    total = jnp.sum(far, axis=1, keepdims=True)
    total = jnp.concatenate([total[:mine] + jnp.sum(near, axis=1, keepdims=True), total[mine:]], axis=0)
    summed = dot(far.astype(BF16), prompt_values)
    summed = jnp.concatenate([summed[:mine] + dot(near.astype(BF16), own_values), summed[mine:]], axis=0)
    some = total > 0.0
    safe = jnp.where(some, total, 1.0)
    result = (summed / safe).astype(BF16)
    level = jnp.where(some, top * scale + jnp.log(safe), NEG_BIG)
    first = level.astype(BF16).astype(F32)
    rest = level - first
    second = rest.astype(BF16).astype(F32)
    third = rest - second
    for i in range(4):
        extra = jnp.zeros((RESP, 128), F32)
        for h in range(2):
            at = slice((2 * i + h) * RESP, (2 * i + h + 1) * RESP)
            outs[i][:, h * HEAD_DIM : (h + 1) * HEAD_DIM] = result[at]
            for n, piece in enumerate((first, second, third)):
                extra = jnp.where(lane == 3 * h + n, piece[at], extra)
        outs[i][:, 256:] = extra.astype(BF16)


def attend(info, rows, queries):
    vmem = pl.BlockSpec(memory_space=pltpu.VMEM)
    return pl.pallas_call(
        attend_kernel,
        in_specs=[pl.BlockSpec(memory_space=pltpu.SMEM)] + [vmem] * 5,
        out_shape=(jax.ShapeDtypeStruct((RESP, 384), BF16),) * 4,
        compiler_params=params(SMALL),
        name="attend",
    )(info, rows, *queries)


def merge_kernel(*refs):
    parts, out_ref = refs[:4], refs[4]
    lane = iota((RESP, 128), 1)
    row, col = iota((128, 128), 0), iota((128, 128), 1)
    order = jnp.where(row == by_device(col), 1.0, 0.0).astype(BF16)
    extras = [part[:, 256:].astype(F32) for part in parts]
    for h in range(2):
        head = slice(h * HEAD_DIM, (h + 1) * HEAD_DIM)
        mine = jnp.logical_and(lane >= 3 * h, lane < 3 * h + 3)
        levels = [jnp.sum(jnp.where(mine, e, 0.0), axis=1, keepdims=True) for e in extras]
        top = functools.reduce(jnp.maximum, levels)
        shares = [jnp.exp(level - top) for level in levels]
        total = functools.reduce(jnp.add, shares)
        pieces = [share * part[:, head].astype(F32) for share, part in zip(shares, parts)]
        mean = (functools.reduce(jnp.add, pieces) / total).astype(BF16)
        out_ref[:, head] = dot(mean, order).astype(BF16)


def merge(parts):
    vmem = pl.BlockSpec(memory_space=pltpu.VMEM)
    return pl.pallas_call(
        merge_kernel,
        in_specs=[vmem] * 4,
        out_shape=jax.ShapeDtypeStruct((RESP, 256), BF16),
        compiler_params=params(SMALL),
        name="merge",
    )(*parts)


def z_of(i, info):
    return (4 * info[CORE_AT]) ^ i


def project_own_kernel(info_ref, own_ref, weight_ref, out_ref):
    for i in range(8):
        at = (2 * z_of(i, info_ref) + info_ref[XL_AT]) * BLOCK
        out_ref[i] = dot(own_ref[...], weight_ref[:, pl.ds(pl.multiple_of(at, BLOCK), BLOCK)])


def project_own(info, own, weight):
    vmem = pl.BlockSpec(memory_space=pltpu.VMEM)
    return pl.pallas_call(
        project_own_kernel,
        in_specs=[pl.BlockSpec(memory_space=pltpu.SMEM)] + [vmem] * 2,
        out_shape=jax.ShapeDtypeStruct((8, RESP, BLOCK), F32),
        compiler_params=params(SMALL),
        cost_estimate=LONG,
        name="project_own",
    )(info, own, weight)


def project_kernel(info_ref, started_ref, other_ref, *refs):
    cross, out_ref = refs[:4], refs[4]
    for i in range(8):
        result = started_ref[i] + dot(other_ref[...], cross[i // 2][:, pl.ds((i % 2) * BLOCK, BLOCK)])
        out_ref[z_of(i, info_ref)] = result.astype(BF16)


def project(info, started, other, cross):
    vmem = pl.BlockSpec(memory_space=pltpu.VMEM)
    return pl.pallas_call(
        project_kernel,
        in_specs=[pl.BlockSpec(memory_space=pltpu.SMEM)] + [vmem] * 6,
        out_shape=jax.ShapeDtypeStruct((8, RESP, BLOCK), BF16),
        compiler_params=params(SMALL),
        name="project",
    )(info, started, other, *cross)


def pick_kernel(info_ref, weight_ref, after_ref, *out_refs):
    for i in range(4):
        at = (2 * z_of(i, info_ref) + 1 - info_ref[XL_AT]) * BLOCK
        columns = weight_ref[:, pl.ds(pl.multiple_of(at, BLOCK), BLOCK)]
        out_refs[i // 2][:, (i % 2) * BLOCK : (i % 2) * BLOCK + BLOCK] = columns


def pick_columns(info, weight, after):
    vmem = pl.BlockSpec(memory_space=pltpu.VMEM)
    return pl.pallas_call(
        pick_kernel,
        in_specs=[pl.BlockSpec(memory_space=pltpu.SMEM)] + [vmem] * 2,
        out_shape=(jax.ShapeDtypeStruct((256, 2 * BLOCK), BF16),) * 2,
        compiler_params=params(SMALL),
        name="pick_columns",
    )(info, weight, after)


def swap(values, axis):
    return lax.all_to_all(values, axis, 0, 0, tiled=False)


def body(
    response_hidden,
    prompt_hidden,
    norm_gain,
    query_weight,
    key_weight,
    value_weight,
    output_weight,
    response_lengths,
    prompt_length,
):
    length = prompt_length[0]
    core, y = lax.axis_index("core"), lax.axis_index("y")
    sample, half, xl = lax.axis_index(SAMPLE), lax.axis_index("zl"), lax.axis_index("xl")
    gain = norm_gain.astype(F32).reshape(16, 1, BLOCK)

    row = jnp.arange(ROWS + RESP, dtype=jnp.int32)[:, None]
    lane = jnp.arange(HEAD_DIM, dtype=jnp.int32)[None, :]
    sample_of = sample - core + (lane >> 6)
    positions = jnp.where(
        row < 128,
        sample_of * PROMPT_ROWS + half * 128 + row,
        jnp.where(row < ROWS, length + half * 32 + row - 128, length + row - ROWS),
    )
    entry = (2 * ((lane >> 2) & 7) + xl) * 8 + 4 * core + (lane & 3)
    entry = jnp.where(row < ROWS, entry, lane)
    still = (row < ROWS) & ((lane & 32) > 0)
    inverse = ROPE_BASE ** (-((entry % HALF).astype(F32) * 2.0 / HEAD_DIM))
    angles = jnp.where(still, 0.0, positions.astype(F32) * inverse)
    trig = jnp.stack([jnp.cos(angles), jnp.sin(angles) * jnp.where(entry < HALF, -1.0, 1.0)])

    info = jnp.stack(
        [core, xl, lax.axis_index(TENSOR), y, lax.axis_index(("xh", "core")), length]
    ).astype(jnp.int32)
    flip = [(0, 1), (1, 0)]

    packed = pack(core.reshape(1), key_weight.T, value_weight.T, response_hidden)
    got = swap(packed, ZRING)
    scaled = scale_rows(info, prompt_hidden, response_hidden, gain)
    beside = lax.ppermute(scaled, "xl", flip)
    crossed = lax.ppermute(scaled, "core", flip), lax.ppermute(beside, "core", flip)
    sent = pick_columns(info, output_weight, scaled)
    early, late = (lax.ppermute(piece, "xl", flip) for piece in sent)
    own_hidden = split(got, (*crossed, early, sent[1], trig))
    other_hidden = lax.ppermute(own_hidden, "xl", flip)
    products = partial_products(info, got, (scaled, beside, *crossed))
    products = swap(products, ZRING)
    queries = queries_of(info, gain, query_weight, trig, own_hidden, other_hidden)
    cross = (early, late, lax.ppermute(early, "core", flip), lax.ppermute(late, "core", flip))
    rows = finish_keys(products, trig, queries)
    rows = swap(rows, KEY_GROUP)

    def along(values, step):
        return lax.ppermute(values, "y", [(i, (i + step) % 4) for i in range(4)])

    around = {step: along(queries, step) for step in (2, 1, 3)}
    pooled = [queries] + [around[step] for step in (1, 2, 3)]
    parts = attend(info, rows, pooled)
    attention = merge([along(parts[step], -step) for step in (2, 1, 3)] + [parts[0]])
    partner = lax.ppermute(attention, "xl", flip)
    partial = project(info, project_own(info, attention, output_weight), partner, cross)
    summed = jnp.sum(swap(partial, ZRING).astype(F32), axis=0)
    live = jnp.arange(RESP, dtype=jnp.int32) < response_lengths[0]
    return jnp.where(live[:, None], summed, 0.0).astype(BF16)


def solution(mesh):
    names = tuple(name for name, _ in PARTS)
    sizes = tuple(size for _, size in PARTS)
    fine = Mesh(mesh.devices.reshape(sizes), names)
    return jax.shard_map(
        body,
        mesh=fine,
        in_specs=(
            P(SAMPLE, TENSOR),
            P(SAMPLE, TENSOR),
            P(),
            P(None, TENSOR),
            P(None, TENSOR),
            P(None, TENSOR),
            P(TENSOR, None),
            P(SAMPLE),
            P(),
        ),
        out_specs=P(SAMPLE, TENSOR),
        check_vma=False,
    )
```
